32 devices in a mesh: pop: 4 (over y, core), col: 8 (over z, x).
Axes of the slice: x: 2, y: 2, z: 4, core: 2. Of those that a mesh axis runs over, the one named last changes fastest.
Arguments:
- tokens: bfloat16 [3584, 4096], P('pop'), may hold values from -6 to 6
- weight: bfloat16 [4096, 16384], P(None, ('col', 'pop')), may hold values from -0.09375 to 0.09375
- old_left: bfloat16 [448, 4, 4096], P('pop', None, 'col'), may hold values from -6 to 6
- old_right: bfloat16 [448, 4, 16384], P('pop', None, 'col'), may hold values from -6 to 6
- selected: int32 [4, 8], P('pop'), may hold values from 0 to 111, as said below
- shaping: float32 [4, 8], P('pop'), may hold values from -3 to 3
- new_left: bfloat16 [448, 4, 4096], P('pop', None, 'col'), may hold values from -6 to 6
- new_right: bfloat16 [448, 4, 16384], P('pop', None, 'col'), may hold values from -6 to 6
Outputs:
- updated: bfloat16 [4096, 16384], P(None, ('col', 'pop'))
- activations: bfloat16 [3584, 16384], P('pop', 'col')
The draws below stay inside these ranges and needn't reach their ends.
Inputs may be any that keep to these rules, and one draw needn't show every extreme that they name: `selected`: each row names 8 different members of its group.
All inputs are finite; a program needn't handle non-finite values.
Results may differ from the reference program's by a relative error of at most 0.0055.
Values may be sent and summed in bfloat16 or wider, within the bound.
No kernel may reach another device: no remote copies, remote signals or barrier semaphores. Data moves between devices by JAX's collectives and lax.ppermute only.
A program may use at most 128 MiB of HBM per device.

```python
import math
import jax
import jax.numpy as jnp
from jax import lax

D = 4096
H = 16384
RANK = 4
TOK_MEM = 8
MEM_DEV = 112
SEL_DEV = 8
MEMBERS = 448
TOKENS = 3584
N_POP = 4


def draw_selected(key, part):
    scores = jax.random.randint(key, (N_POP, MEM_DEV), 0, 2 ** 20, dtype=jnp.int32)
    scores = scores * MEM_DEV + jnp.arange(MEM_DEV, dtype=jnp.int32)[None, :]
    order = jnp.argsort(scores, axis=1, stable=True)
    return order[:, :SEL_DEV].astype(jnp.int32)


def block_levels(key, dims, shards, least, largest):
    gain, own = 1.0, jax.random.fold_in(key, 6)
    for position, blocks in shards:
        heights = jnp.exp(jax.random.uniform(jax.random.fold_in(own, position), (blocks,), jnp.float32, least / len(shards), largest / len(shards)))
        gain = gain * jnp.repeat(heights, dims[position] // blocks).reshape([-1 if axis == position else 1 for axis in range(len(dims))])
    return gain


def scatter_about(own_key, extent, spread, bound, cuts=(), held_as=jnp.bfloat16):
    array = spread * jax.random.normal(own_key, extent, jnp.float32)
    if cuts:
        array = array * block_levels(own_key, extent, cuts, -0.22, 0.18)
    return jnp.clip(array, -bound, bound).astype(held_as)


def setup_inputs(seed: int = 0) -> dict:
    splits = jax.random.split(jax.random.key(seed), 9)
    return {
        "tokens": scatter_about(splits[0], (TOKENS, D), 1.0, 6.0, ((0, 4),)),
        "weight": scatter_about(splits[1], (D, H), D ** -0.5, 0.09375, ((1, 32),)),
        "old_left": scatter_about(splits[2], (MEMBERS, RANK, D), 1.0, 6.0, ((0, 4), (2, 8))),
        "old_right": scatter_about(splits[3], (MEMBERS, RANK, H), 1.0, 6.0, ((0, 4), (2, 8))),
        "selected": draw_selected(jax.random.fold_in(splits[8], 71), 0),
        "shaping": scatter_about(splits[5], (N_POP, SEL_DEV), 0.5, 3.0, ((0, 4),), jnp.float32),
        "new_left": scatter_about(splits[6], (MEMBERS, RANK, D), 1.0, 6.0, ((0, 4), (2, 8))),
        "new_right": scatter_about(splits[7], (MEMBERS, RANK, H), 1.0, 6.0, ((0, 4), (2, 8))),
    }


noise_scale = 0.5

def reference(tokens, weight, old_left, old_right, selected, shaping, new_left, new_right):
    members = (jnp.arange(N_POP, dtype=jnp.int32)[:, None] * MEM_DEV + selected.astype(jnp.int32)).reshape(-1)
    factor = 1.0 / math.sqrt(D * RANK * SEL_DEV * N_POP)
    weights_here = shaping.reshape(-1) * factor
    scaled_left = (old_left[members].astype(jnp.float32) * weights_here[:, None, None]).astype(jnp.bfloat16)
    chosen_right = old_right[members]
    delta = jnp.dot(scaled_left.reshape(-1, D).T, chosen_right.reshape(-1, H), preferred_element_type=jnp.float32)
    updated = (weight.astype(jnp.float32) + delta).astype(jnp.bfloat16)
    side_scale = noise_scale / math.sqrt(D * RANK)

    def group_forward(args):
        rows, lefts, rights = args
        base = jnp.dot(rows, updated, preferred_element_type=jnp.float32)
        per_member = rows.reshape(MEM_DEV, TOK_MEM, D).astype(jnp.float32)
        proj = jnp.einsum('mtd,mrd->mtr', per_member, lefts.astype(jnp.float32), precision=lax.Precision.HIGHEST).astype(jnp.bfloat16)
        side = jnp.einsum('mtr,mrh->mth', proj.astype(jnp.float32), rights.astype(jnp.float32), precision=lax.Precision.HIGHEST).reshape(MEM_DEV * TOK_MEM, H)
        pre = base + side_scale * side
        return (jnp.maximum(pre, 0.0) ** 2).astype(jnp.bfloat16)
    outputs = lax.map(group_forward, (tokens.reshape(N_POP, MEM_DEV * TOK_MEM, D), new_left.reshape(N_POP, MEM_DEV, RANK, D), new_right.reshape(N_POP, MEM_DEV, RANK, H)))
    return (updated, outputs.reshape(TOKENS, H))
```

```python
import functools
import math

import jax
import jax.numpy as jnp
from jax import lax
from jax.experimental import pallas as pl
from jax.experimental.pallas import tpu as pltpu
from jax.sharding import PartitionSpec as P

noise_scale = 0.5
PIECES = (1, 1, 3, 8, 2, 1)
LIMIT = 20 * 2**20
WIDE = 58 * 2**20


def params():
    return pltpu.CompilerParams(dimension_semantics=("arbitrary",), vmem_limit_bytes=LIMIT)


def cost():
    return pl.CostEstimate(flops=1, bytes_accessed=1, transcendentals=0)


def swap(array, axis, bit):
    return lax.ppermute(array, axis, [(i, i ^ bit) for i in range(lax.axis_size(axis))])


def bits(size, least=1):
    bit = least
    while bit < size:
        yield bit
        bit *= 2


MARK = jax.ShapeDtypeStruct((8, 128), jnp.float32)


def vmem():
    return pl.BlockSpec(memory_space=pltpu.VMEM)


def anywhere():
    return pl.BlockSpec(memory_space=pl.ANY)


def gate_kernel(mark_at, *refs):
    refs[mark_at][...] = jnp.zeros(MARK.shape, MARK.dtype)


def gate(array, *after):
    return pl.pallas_call(
        functools.partial(gate_kernel, len(after) + 2),
        in_specs=[anywhere()] * (1 + len(after)),
        out_specs=[anywhere(), vmem()],
        out_shape=[jax.ShapeDtypeStruct(array.shape, array.dtype), MARK],
        input_output_aliases={0: 0},
        compiler_params=pltpu.CompilerParams(vmem_limit_bytes=2**20),
        cost_estimate=cost(),
    )(array, *after)


def cut_kernel(start, wt, after, out, mark, sem):
    copy = pltpu.make_async_copy(wt.at[pl.ds(start, out.shape[0])], out, sem)
    copy.start()
    copy.wait()
    mark[...] = jnp.zeros(MARK.shape, MARK.dtype)


def cut(weight, start, depth, after):
    return pl.pallas_call(
        functools.partial(cut_kernel, start),
        in_specs=[anywhere()] * 2,
        out_specs=[vmem()] * 2,
        out_shape=[jax.ShapeDtypeStruct((depth, weight.shape[1]), weight.dtype), MARK],
        scratch_shapes=[pltpu.SemaphoreType.DMA],
        compiler_params=pltpu.CompilerParams(vmem_limit_bytes=WIDE),
        cost_estimate=cost(),
    )(weight, after)


def copy_kernel(wt, after, out):
    out[...] = wt[...]


def copy_of(weight, after):
    depth, width = weight.shape
    block = pl.BlockSpec((depth // 4, width), lambda k: (k, 0))
    return pl.pallas_call(
        copy_kernel,
        grid=(4,),
        in_specs=[block, anywhere()],
        out_specs=block,
        out_shape=jax.ShapeDtypeStruct(weight.shape, weight.dtype),
        compiler_params=pltpu.CompilerParams(
            dimension_semantics=("arbitrary",), vmem_limit_bytes=WIDE
        ),
        cost_estimate=cost(),
    )(weight, after)


def pick_kernel(factor, picked, shaping, lefts, rights, wt, packed, left, right, mark, sem):
    count, rank, _ = lefts.shape
    chosen, width = picked.shape[1], packed.shape[1]
    tall = chosen * rank
    first = tall * (left.shape[1] + right.shape[1]) // width
    depth = packed.shape[0] - first
    copy = pltpu.make_async_copy(wt.at[pl.ds(0, depth)], packed.at[pl.ds(first, depth)], sem)
    copy.start()
    scaled, plain = [], []
    for slot in range(chosen):
        member = picked[0, slot]
        scale = shaping[0, slot] * factor
        scaled.append(lefts[member].astype(jnp.float32) * scale)
        plain.append(rights[member].astype(jnp.float32))
    scaled = jnp.concatenate(scaled, 0).astype(jnp.bfloat16)
    plain = jnp.concatenate(plain, 0).astype(jnp.bfloat16)
    left[...] = scaled
    right[...] = plain
    at = 0
    for whole in (scaled, plain):
        for block in range(whole.shape[1] // width):
            packed[at : at + tall, :] = whole[:, block * width : (block + 1) * width]
            at += tall
    mark[...] = jnp.zeros(MARK.shape, MARK.dtype)
    copy.wait()


def pick(factor, selected, shaping, old_left, old_right, weight, depth):
    tall = selected.shape[1] * old_left.shape[1]
    slab, wide, width = old_left.shape[2], old_right.shape[2], weight.shape[1]
    rows = tall * (slab + wide) // width + depth
    return pl.pallas_call(
        functools.partial(pick_kernel, factor),
        in_specs=[pl.BlockSpec(memory_space=pltpu.SMEM)] * 2 + [vmem()] * 2 + [anywhere()],
        out_specs=[vmem()] * 4,
        out_shape=[
            jax.ShapeDtypeStruct((rows, width), weight.dtype),
            jax.ShapeDtypeStruct((tall, slab), weight.dtype),
            jax.ShapeDtypeStruct((tall, wide), weight.dtype),
            MARK,
        ],
        scratch_shapes=[pltpu.SemaphoreType.DMA],
        compiler_params=pltpu.CompilerParams(vmem_limit_bytes=WIDE),
        cost_estimate=cost(),
    )(selected, shaping, old_left, old_right, weight)


def unpack(packed, tall, slab, wide):
    width = packed.shape[1]
    blocks = [slab // width, wide // width]
    got, at = [], 0
    for count in blocks:
        got.append(
            jnp.concatenate([packed[at + tall * i : at + tall * (i + 1)] for i in range(count)], 1)
        )
        at += tall * count
    return (*got, packed[at:])


def mine(shape, rank, each):
    row = lax.broadcasted_iota(jnp.int32, shape, 0)
    token = lax.broadcasted_iota(jnp.int32, shape, 1)
    return lax.div(row, rank) == lax.div(token, each)


def proj_kernel(rank, each, where, left, tok, after, out):
    full = lax.dot_general(
        left[...], tok[...], (((1,), (1,)), ((), ())), preferred_element_type=jnp.float32
    )
    full = jnp.where(mine(full.shape, rank, each), full, 0.0)
    out[...] = full.reshape(-1, *out.shape).sum(0)


def project(tokens, lefts, rank, each, where, after):
    rows, slab = tokens.shape[0], lefts.shape[1]
    return pl.pallas_call(
        functools.partial(proj_kernel, rank, each),
        grid_spec=pltpu.PrefetchScalarGridSpec(
            num_scalar_prefetch=1,
            grid=(1,),
            in_specs=[
                pl.BlockSpec(lefts.shape, lambda k, at: (0, 0)),
                pl.BlockSpec((rows, slab), lambda k, at: (0, at[1])),
                pl.BlockSpec(memory_space=pl.ANY),
            ],
            out_specs=pl.BlockSpec((2 * rank, rows), lambda k, at: (0, 0)),
        ),
        out_shape=jax.ShapeDtypeStruct((2 * rank, rows), jnp.float32),
        compiler_params=params(),
        cost_estimate=cost(),
    )(where, lefts, tokens, after)


def turn_kernel(where, left, out):
    out[...] = left[...].T


def turn(left, where):
    blocks, sels, slab = left.shape
    return pl.pallas_call(
        turn_kernel,
        grid_spec=pltpu.PrefetchScalarGridSpec(
            num_scalar_prefetch=1,
            grid=(blocks,),
            in_specs=[pl.BlockSpec((None, sels, slab), lambda k, at: (k ^ at[1], 0, 0))],
            out_specs=pl.BlockSpec((slab, sels), lambda k, at: (k, 0)),
        ),
        out_shape=jax.ShapeDtypeStruct((blocks * slab, sels), left.dtype),
        compiler_params=params(),
        cost_estimate=cost(),
    )(where, left)


def spread_kernel(rank, each, proj, out):
    narrow = proj[...].astype(jnp.bfloat16).astype(jnp.float32)
    full = jnp.tile(narrow, (out.shape[1] // narrow.shape[0], 1))
    out[...] = jnp.where(mine(full.shape, rank, each), full, 0.0).T.astype(jnp.bfloat16)


def spread_out(proj, members, rank, each):
    return pl.pallas_call(
        functools.partial(spread_kernel, rank, each),
        in_specs=[pl.BlockSpec(memory_space=pltpu.VMEM)],
        out_specs=pl.BlockSpec(memory_space=pltpu.VMEM),
        out_shape=jax.ShapeDtypeStruct((proj.shape[1], members * rank), jnp.bfloat16),
        compiler_params=pltpu.CompilerParams(vmem_limit_bytes=LIMIT),
        cost_estimate=cost(),
    )(proj)


def columns(ref, at, width):
    return ref[:, pl.ds(pl.multiple_of(at * width, width), width)]


def refresh(wt, left, right):
    delta = jnp.dot(left, right, preferred_element_type=jnp.float32)
    return (wt.astype(jnp.float32) + delta).astype(jnp.bfloat16)


def finish(total):
    return (jnp.maximum(total, 0.0) ** 2).astype(jnp.bfloat16)


def begin(scale, spread, rights, at, width):
    side = jnp.dot(spread[...], columns(rights, at, width), preferred_element_type=jnp.float32)
    return scale * side


def full_kernel(scale, keep, begun, where, tok, wt, left, right, spread, rights, *refs):
    out, mark, held = refs[1 if begun else 2], refs[-2], refs[-1]
    width, unit = wt.shape[1], wt.shape[0]
    step = pl.program_id(0)

    @pl.when(step == 0)
    def _():
        mark[...] = jnp.zeros(MARK.shape, MARK.dtype)
        held[...] = begin(scale, spread, rights, where[0], width)

    at = pl.multiple_of(step * unit, unit)
    fresh = refresh(wt[...], left[pl.ds(at, unit), :], columns(right, where[0], width))
    if keep:
        refs[-3][...] = fresh
    held[...] += jnp.dot(tok[:, pl.ds(at, unit)], fresh, preferred_element_type=jnp.float32)

    @pl.when(step == pl.num_programs(0) - 1)
    def _():
        out[...] = finish(held[...])


def first_kernel(scale, start, where, tok, wt, left, right, spread, rights, after, out):
    width, unit = wt.shape[1], wt.shape[0]
    fresh = refresh(wt[...], left[start : start + unit, :], columns(right, where[0], width))
    out[...] = begin(scale, spread, rights, where[0], width) + jnp.dot(
        tok[:, start : start + unit], fresh, preferred_element_type=jnp.float32
    )


def middle_kernel(start, where, tok, wt, left, right, before, after, out):
    width, unit = wt.shape[1], wt.shape[0]
    fresh = refresh(wt[...], left[start : start + unit, :], columns(right, where[0], width))
    out[...] = before[...] + jnp.dot(
        tok[:, start : start + unit], fresh, preferred_element_type=jnp.float32
    )


def last_kernel(start, where, tok, wt, left, right, before, after, acts, out, kept):
    width, unit = wt.shape[1], wt.shape[0]
    step, part = pl.program_id(0), out.shape[0]

    @pl.when(step == 0)
    def _():
        kept[...] = refresh(
            wt[...], left[start : start + unit, :], columns(right, where[0], width)
        )

    rows = pl.ds(pl.multiple_of(step * part, part), part)
    out[...] = finish(
        before[rows, :]
        + jnp.dot(
            tok[rows, start : start + unit], kept[...], preferred_element_type=jnp.float32
        )
    )


def call(kernel, where, grid, specs, args, out_specs, out_shape, aliases=None, scratch=()):
    return pl.pallas_call(
        kernel,
        grid_spec=pltpu.PrefetchScalarGridSpec(
            num_scalar_prefetch=1,
            grid=grid,
            in_specs=specs,
            out_specs=out_specs,
            scratch_shapes=list(scratch),
        ),
        out_shape=out_shape,
        input_output_aliases=aliases or {},
        compiler_params=params(),
        cost_estimate=cost(),
    )(where, *args)


def run_block(where, tokens, wt, left, right, start, scale, spread, rights, acts, before, after, keep):
    rows = tokens.shape[0]
    depth, width = wt.shape
    first, last, begun = start == 0, acts is not None, isinstance(acts, tuple)
    held = pl.BlockSpec(memory_space=pltpu.VMEM)
    anywhere = pl.BlockSpec(memory_space=pl.ANY)
    tile = pl.BlockSpec((rows, width), lambda k, at: (0, at[0]))
    if first and last:
        unit = depth // 4
        block = pl.BlockSpec((unit, width), lambda k, at: (k, 0))
        specs, args = [held, block] + [held] * 4, [tokens, wt, left, right, spread, rights]
        specs, args = specs + [anywhere], args + [after]
        aliases = {}
        if not begun:
            specs, args = specs + [anywhere], args + [acts]
            aliases = {len(args): 0}
        shape = acts if begun else acts.shape
        out_shape, out_specs = [jax.ShapeDtypeStruct(shape, jnp.bfloat16)], [tile]
        if keep:
            out_shape.append(jax.ShapeDtypeStruct((depth, width), jnp.bfloat16))
            out_specs.append(block)
        out_shape.append(MARK)
        out_specs.append(vmem())
        return call(
            functools.partial(full_kernel, scale, keep, begun),
            where, (4,), specs, args, out_specs, out_shape, aliases,
            [pltpu.VMEM((rows, width), jnp.float32)],
        )
    sums = jax.ShapeDtypeStruct((rows, width), jnp.float32)
    if first:
        return call(
            functools.partial(first_kernel, scale, start),
            where, (1,), [held] * 6 + [anywhere],
            [tokens, wt, left, right, spread, rights, after], held, sums,
        )
    if not last:
        return call(
            functools.partial(middle_kernel, start),
            where, (1,), [held] * 5 + [anywhere],
            [tokens, wt, left, right, before, after], held, sums, {5: 0},
        )
    part = rows // 4
    return call(
        functools.partial(last_kernel, start),
        where, (4,), [held] * 5 + [anywhere] * 2,
        [tokens, wt, left, right, before, after, acts],
        pl.BlockSpec((part, width), lambda k, at: (k, at[0])),
        jax.ShapeDtypeStruct(acts.shape, jnp.bfloat16), {7: 0},
        [pltpu.VMEM((depth, width), jnp.bfloat16)],
    )


def local(tokens, weight, old_left, old_right, selected, shaping, new_left, new_right):
    groups = lax.axis_size("pop")
    me = lax.axis_index("pop")
    spot = lax.axis_index("col")
    depth, width = weight.shape
    members, rank, slab = new_left.shape
    rows = tokens.shape[0]
    each = rows // members
    count = selected.shape[1]
    scale = noise_scale / math.sqrt(depth * rank)
    grain = depth // sum(PIECES)
    chips = groups // 2
    where = jnp.stack([me, spot]).astype(jnp.int32)

    plan = []
    hops = [chips // 2] + [hop for hop in range(1, chips) if hop != chips // 2]
    for hop in hops:
        at = 0
        for piece in PIECES if hop == hops[-1] else (sum(PIECES),):
            plan.append((hop, at * grain, piece * grain))
            at += piece

    def send(index, piece):
        turn = [(p, (p + 2 * plan[index][0]) % groups) for p in range(groups)]
        return lax.ppermute(piece, "pop", turn)

    factor = 1.0 / math.sqrt(depth * rank * count * groups)
    packed, left, right, mark = pick(
        factor, selected, shaping, old_left, old_right, weight, plan[0][2]
    )
    arrived = [send(0, packed)]
    piece, mark = cut(weight, *plan[1][1:], mark)
    arrived.append(send(1, piece))
    proj = project(tokens, new_left.reshape(-1, slab), rank, each, where, mark)
    tall = count * rank
    lefts, rights, arrived[0] = unpack(arrived[0], tall, slab, old_right.shape[2])
    left, right = jnp.concatenate([left, lefts], 0), jnp.concatenate([right, rights], 0)
    for bit in bits(chips, 2):
        left = jnp.concatenate([left, swap(left, "pop", bit)], 0)
        right = jnp.concatenate([right, swap(right, "pop", bit)], 0)
    pieces = [weight[start : start + size] for _, start, size in plan[2:]]
    piece, mark = gate(pieces[0], mark)
    arrived.append(send(2, piece))
    own = copy_of(weight, left)
    right = jnp.concatenate([right, swap(right, "pop", 1)], 0)
    left = left[None]
    for turns, bit in enumerate(bits(lax.axis_size("col"))):
        left = jnp.concatenate([left, swap(left, "col", bit)], 0)
        proj = proj + swap(proj, "col", bit)
        if turns == 0:
            arrived[1], mark = gate(arrived[1], left)
            piece, mark = gate(pieces[1], mark)
            arrived.append(send(3, piece))
            left, _ = gate(left, mark)
    arrived[2], mark = gate(arrived[2], left)
    piece, mark = gate(pieces[2], mark)
    arrived.append(send(4, piece))
    left, _ = gate(left, mark)
    own, mark = gate(own, right, proj)
    sibling = swap(own, "pop", 1)
    left = turn(jnp.concatenate([left, swap(left, "pop", 1)], 1), where)
    spread = spread_out(proj, members, rank, each)
    rights = new_right.reshape(members * rank, -1)

    def run(block, wt, start, before, acts, after, keep=False):
        return run_block(
            jnp.reshape(block, (1,)).astype(jnp.int32),
            tokens, wt, left, right, start, scale, spread, rights, acts, before, after, keep,
        )

    narrow = width % 128 != 0
    core = lax.rem(me, 2)

    def pair(own, other):
        return jnp.where(
            core == 0, jnp.concatenate([own, other], 1), jnp.concatenate([other, own], 1)
        )

    whole = (rows, width * groups)
    if narrow:
        acts, both, done = run(me // 2, pair(weight, sibling), 0, None, whole, where, keep=True)
        updated = lax.dynamic_slice_in_dim(both, core * width, width, 1)
    else:
        acts, updated, done = run(me, weight, 0, None, whole, where, keep=True)
    crossed = [None] * len(plan)

    def arrive(index, after):
        arrived[index], mark = gate(arrived[index], after)
        if index + 2 < len(plan):
            piece, mark = gate(pieces[index], mark)
            arrived.append(send(index + 2, piece))

    def cross(index, after):
        arrived[index], _ = gate(arrived[index], after)
        crossed[index] = swap(arrived[index], "pop", 1)

    cross(0, done)
    cross(1, done)
    if not narrow:
        acts, done = run(me ^ 1, sibling, 0, None, acts, done)
    cross(2, done)
    for index, (hop, start, size) in enumerate(plan):
        if index > 2:
            arrive(index, done)
            cross(index, done)
        part, other = arrived[index], crossed[index]
        if start == 0:
            sums = [None, None]
        ends = start + size == depth
        source = lax.rem(me - 2 * hop + 2 * groups, groups)
        tasks = ((source, part), (source ^ 1, other))
        if narrow:
            tasks = ((source // 2, pair(part, other)),)
        for side, (block, wt) in enumerate(tasks):
            got = run(block, wt, start, sums[side], acts if ends else None, done)
            if not ends:
                sums[side] = done = got
            elif start == 0:
                acts, done = got
            else:
                acts = got
    return updated, acts


def solution(mesh):
    placed = (
        P("pop", None),
        P(None, ("col", "pop")),
        P("pop", None, "col"),
        P("pop", None, "col"),
        P("pop", None),
        P("pop", None),
        P("pop", None, "col"),
        P("pop", None, "col"),
    )
    return jax.shard_map(
        local,
        mesh=mesh,
        in_specs=placed,
        out_specs=(P(None, ("col", "pop")), P("pop", "col")),
        check_vma=False,
    )
```

```python
import functools
import math

import jax
import jax.numpy as jnp
from jax import lax
from jax.experimental import pallas as pl
from jax.experimental.pallas import tpu as pltpu
from jax.sharding import PartitionSpec as P

noise_scale = 0.5
PIECES = (1, 4, 9, 2)
LIMIT = 20 * 2**20
WIDE = 58 * 2**20


def params(limit=LIMIT):
    return pltpu.CompilerParams(dimension_semantics=("arbitrary",), vmem_limit_bytes=limit)


def cost():
    return pl.CostEstimate(flops=1, bytes_accessed=1, transcendentals=0)


def swap(array, axis, bit):
    return lax.ppermute(array, axis, [(i, i ^ bit) for i in range(lax.axis_size(axis))])


def bits(size, least=1):
    bit = least
    while bit < size:
        yield bit
        bit *= 2


MARK = jax.ShapeDtypeStruct((8, 128), jnp.float32)


def vmem():
    return pl.BlockSpec(memory_space=pltpu.VMEM)


def anywhere():
    return pl.BlockSpec(memory_space=pl.ANY)


def gate_kernel(mark_at, *refs):
    refs[mark_at][...] = jnp.zeros(MARK.shape, MARK.dtype)


def gate(array, *after):
    return pl.pallas_call(
        functools.partial(gate_kernel, len(after) + 2),
        in_specs=[anywhere()] * (1 + len(after)),
        out_specs=[anywhere(), vmem()],
        out_shape=[jax.ShapeDtypeStruct(array.shape, array.dtype), MARK],
        input_output_aliases={0: 0},
        compiler_params=pltpu.CompilerParams(vmem_limit_bytes=2**20),
        cost_estimate=cost(),
    )(array, *after)


def cut_kernel(start, wt, after, out, mark, sem):
    copy = pltpu.make_async_copy(wt.at[pl.ds(start, out.shape[0])], out, sem)
    copy.start()
    copy.wait()
    mark[...] = jnp.zeros(MARK.shape, MARK.dtype)


def cut(weight, start, depth, after):
    return pl.pallas_call(
        functools.partial(cut_kernel, start),
        in_specs=[anywhere()] * 2,
        out_specs=[vmem()] * 2,
        out_shape=[jax.ShapeDtypeStruct((depth, weight.shape[1]), weight.dtype), MARK],
        scratch_shapes=[pltpu.SemaphoreType.DMA],
        compiler_params=pltpu.CompilerParams(vmem_limit_bytes=WIDE - 2 * depth * weight.shape[1]),
        cost_estimate=cost(),
    )(weight, after)


def pick_kernel(
    factor, picked, shaping, lefts, rights, after, packed, left, right, mark, some_left, some_right, sems
):
    chosen, width = picked.shape[1], packed.shape[1]
    tall = chosen * lefts.shape[1]
    copies = []
    for slot in range(chosen):
        member = picked[0, slot]
        for source, kept in ((lefts, some_left), (rights, some_right)):
            sem = sems.at[len(copies)]
            copies.append(pltpu.make_async_copy(source.at[member], kept.at[slot], sem))
    for copy in copies:
        copy.start()
    for copy in copies:
        copy.wait()
    scaled, plain = [], []
    for slot in range(chosen):
        scale = shaping[0, slot] * factor
        scaled.append(some_left[slot].astype(jnp.float32) * scale)
        plain.append(some_right[slot].astype(jnp.float32))
    scaled = jnp.concatenate(scaled, 0).astype(jnp.bfloat16)
    plain = jnp.concatenate(plain, 0).astype(jnp.bfloat16)
    left[...] = scaled
    right[...] = plain
    at = 0
    for whole in (scaled, plain):
        for block in range(whole.shape[1] // width):
            packed[at : at + tall, :] = whole[:, block * width : (block + 1) * width]
            at += tall
    mark[...] = jnp.zeros(MARK.shape, MARK.dtype)


def pick(factor, selected, shaping, old_left, old_right, width, after):
    chosen, rank = selected.shape[1], old_left.shape[1]
    tall = chosen * rank
    slab, wide, kind = old_left.shape[2], old_right.shape[2], old_left.dtype
    return pl.pallas_call(
        functools.partial(pick_kernel, factor),
        in_specs=[pl.BlockSpec(memory_space=pltpu.SMEM)] * 2 + [anywhere()] * 3,
        out_specs=[vmem()] * 4,
        out_shape=[
            jax.ShapeDtypeStruct((tall * (slab + wide) // width, width), kind),
            jax.ShapeDtypeStruct((tall, slab), kind),
            jax.ShapeDtypeStruct((tall, wide), kind),
            MARK,
        ],
        scratch_shapes=[
            pltpu.VMEM((chosen, rank, slab), kind),
            pltpu.VMEM((chosen, rank, wide), kind),
            pltpu.SemaphoreType.DMA((2 * chosen,)),
        ],
        compiler_params=pltpu.CompilerParams(vmem_limit_bytes=WIDE),
        cost_estimate=cost(),
    )(selected, shaping, old_left, old_right, after)


def unpack(packed, tall, slab, wide):
    width = packed.shape[1]
    blocks = [slab // width, wide // width]
    got, at = [], 0
    for count in blocks:
        got.append(
            jnp.concatenate([packed[at + tall * i : at + tall * (i + 1)] for i in range(count)], 1)
        )
        at += tall * count
    return got


def mine(shape, rank, each):
    row = lax.broadcasted_iota(jnp.int32, shape, 0)
    token = lax.broadcasted_iota(jnp.int32, shape, 1)
    return lax.div(row, rank) == lax.div(token, each)


def proj_kernel(rank, each, where, left, tok, after, out):
    full = lax.dot_general(
        left[...], tok[...], (((1,), (1,)), ((), ())), preferred_element_type=jnp.float32
    )
    full = jnp.where(mine(full.shape, rank, each), full, 0.0)
    out[...] = full.reshape(-1, *out.shape).sum(0)


def project(tokens, lefts, rank, each, where, after):
    rows, slab = tokens.shape[0], lefts.shape[1]
    return pl.pallas_call(
        functools.partial(proj_kernel, rank, each),
        grid_spec=pltpu.PrefetchScalarGridSpec(
            num_scalar_prefetch=1,
            grid=(1,),
            in_specs=[
                pl.BlockSpec(lefts.shape, lambda k, at: (0, 0)),
                pl.BlockSpec((rows, slab), lambda k, at: (0, at[1])),
                pl.BlockSpec(memory_space=pl.ANY),
            ],
            out_specs=pl.BlockSpec((2 * rank, rows), lambda k, at: (0, 0)),
        ),
        out_shape=jax.ShapeDtypeStruct((2 * rank, rows), jnp.float32),
        compiler_params=params(WIDE),
        cost_estimate=cost(),
    )(where, lefts, tokens, after)


def turn_kernel(where, left, out):
    out[...] = left[...].T


def turn(left, where):
    blocks, sels, slab = left.shape
    return pl.pallas_call(
        turn_kernel,
        grid_spec=pltpu.PrefetchScalarGridSpec(
            num_scalar_prefetch=1,
            grid=(blocks,),
            in_specs=[pl.BlockSpec((None, sels, slab), lambda k, at: (k ^ at[1], 0, 0))],
            out_specs=pl.BlockSpec((slab, sels), lambda k, at: (k, 0)),
        ),
        out_shape=jax.ShapeDtypeStruct((blocks * slab, sels), left.dtype),
        compiler_params=params(),
        cost_estimate=cost(),
    )(where, left)


def spread_kernel(rank, each, proj, out):
    narrow = proj[...].astype(jnp.bfloat16).astype(jnp.float32)
    full = jnp.tile(narrow, (out.shape[1] // narrow.shape[0], 1))
    out[...] = jnp.where(mine(full.shape, rank, each), full, 0.0).T.astype(jnp.bfloat16)


def spread_out(proj, members, rank, each):
    return pl.pallas_call(
        functools.partial(spread_kernel, rank, each),
        in_specs=[pl.BlockSpec(memory_space=pltpu.VMEM)],
        out_specs=pl.BlockSpec(memory_space=pltpu.VMEM),
        out_shape=jax.ShapeDtypeStruct((proj.shape[1], members * rank), jnp.bfloat16),
        compiler_params=pltpu.CompilerParams(vmem_limit_bytes=LIMIT),
        cost_estimate=cost(),
    )(proj)


def columns(ref, at, width):
    return ref[:, pl.ds(pl.multiple_of(at * width, width), width)]


def refresh(wt, left, right):
    delta = jnp.dot(left, right, preferred_element_type=jnp.float32)
    return (wt.astype(jnp.float32) + delta).astype(jnp.bfloat16)


def finish(total):
    return (jnp.maximum(total, 0.0) ** 2).astype(jnp.bfloat16)


def begin(scale, spread, rights):
    return scale * jnp.dot(spread, rights, preferred_element_type=jnp.float32)


def full_kernel(scale, keep, begun, where, tok, wt, left, right, spread, rights, *refs):
    out, mark, held = refs[1 if begun else 2], refs[-2], refs[-1]
    step = pl.program_id(0)

    @pl.when(step == 0)
    def _():
        mark[...] = jnp.zeros(MARK.shape, MARK.dtype)
        held[...] = begin(scale, spread[...], rights[...])

    fresh = refresh(wt[...], left[...], right[...])
    if keep:
        refs[-3][...] = fresh
    held[...] += jnp.dot(tok[...], fresh, preferred_element_type=jnp.float32)

    @pl.when(step == pl.num_programs(0) - 1)
    def _():
        out[...] = finish(held[...])


def product(start, where, tok, wt, left, right):
    unit, width = wt.shape
    fresh = refresh(wt[...], left[start : start + unit, :], columns(right, where[0], width))

    def rows(at, size):
        some = tok[at : at + size, start : start + unit]
        return jnp.dot(some, fresh, preferred_element_type=jnp.float32)

    return rows


def sum_kernel(scale, start, where, tok, wt, left, right, *refs):
    out = refs[-1]
    if start == 0:
        before = begin(scale, refs[0][...], columns(refs[1], where[0], wt.shape[1]))
    else:
        before = refs[0][...]
    out[...] = before + product(start, where, tok, wt, left, right)(0, tok.shape[0])


def last_kernel(start, where, tok, wt, left, right, before, acts, out, kept, sems):
    width = wt.shape[1]
    got = product(start, where, tok, wt, left, right)
    part = kept.shape[0] // 2
    place = pl.ds(pl.multiple_of(where[0] * width, width), width)
    copies = []
    for half in range(2):
        rows = pl.ds(half * part, part)
        kept[rows, :] = finish(before[rows, :] + got(half * part, part))
        copies.append(pltpu.make_async_copy(kept.at[rows], out.at[rows, place], sems.at[half]))
        copies[-1].start()
    for copy in copies:
        copy.wait()


def call(
    kernel, where, grid, specs, args, out_specs, out_shape, aliases=None, scratch=(), limit=LIMIT
):
    return pl.pallas_call(
        kernel,
        grid_spec=pltpu.PrefetchScalarGridSpec(
            num_scalar_prefetch=1,
            grid=grid,
            in_specs=specs,
            out_specs=out_specs,
            scratch_shapes=list(scratch),
        ),
        out_shape=out_shape,
        input_output_aliases=aliases or {},
        compiler_params=params(limit),
        cost_estimate=cost(),
    )(where, *args)


def run_block(where, tokens, wt, left, right, start, scale, spread, rights, acts, before, after, keep):
    rows = tokens.shape[0]
    depth, width = wt.shape
    first, last, begun = start == 0, acts is not None, isinstance(acts, tuple)
    tile = pl.BlockSpec((rows, width), lambda k, at: (0, at[0]))
    if first and last:
        unit = depth // 4
        block = pl.BlockSpec((unit, width), lambda k, at: (k, 0))
        specs = [
            pl.BlockSpec((rows, unit), lambda k, at: (0, k)),
            block,
            pl.BlockSpec((unit, left.shape[1]), lambda k, at: (k, 0)),
            pl.BlockSpec((right.shape[0], width), lambda k, at: (0, at[0])),
            pl.BlockSpec(spread.shape, lambda k, at: (0, 0)),
            pl.BlockSpec((rights.shape[0], width), lambda k, at: (0, at[0])),
            anywhere(),
        ]
        args = [tokens, wt, left, right, spread, rights, after]
        aliases = {}
        if not begun:
            specs, args = specs + [anywhere()], args + [acts]
            aliases = {len(args): 0}
        shape = acts if begun else acts.shape
        out_shape, out_specs = [jax.ShapeDtypeStruct(shape, jnp.bfloat16)], [tile]
        if keep:
            out_shape.append(jax.ShapeDtypeStruct((depth, width), jnp.bfloat16))
            out_specs.append(block)
        out_shape.append(MARK)
        out_specs.append(vmem())
        return call(
            functools.partial(full_kernel, scale, keep, begun),
            where, (4,), specs, args, out_specs, out_shape, aliases,
            [pltpu.VMEM((rows, width), jnp.float32)], WIDE,
        )
    if not last:
        extra = [spread, rights] if first else [before]
        return call(
            functools.partial(sum_kernel, scale, start),
            where, (1,), [vmem()] * (4 + len(extra)) + [anywhere()],
            [tokens, wt, left, right, *extra, after], vmem(),
            jax.ShapeDtypeStruct((rows, width), jnp.float32), {} if first else {5: 0},
        )
    return call(
        functools.partial(last_kernel, start),
        where, (1,), [vmem()] * 5 + [anywhere()],
        [tokens, wt, left, right, before, acts], anywhere(),
        jax.ShapeDtypeStruct(acts.shape, jnp.bfloat16), {6: 0},
        [pltpu.VMEM((rows, width), jnp.bfloat16), pltpu.SemaphoreType.DMA((2,))],
    )


def local(tokens, weight, old_left, old_right, selected, shaping, new_left, new_right):
    groups = lax.axis_size("pop")
    me = lax.axis_index("pop")
    spot = lax.axis_index("col")
    depth, width = weight.shape
    members, rank, slab = new_left.shape
    rows = tokens.shape[0]
    each = rows // members
    count = selected.shape[1]
    scale = noise_scale / math.sqrt(depth * rank)
    grain = depth // sum(PIECES)
    chips = groups // 2
    where = jnp.stack([me, spot]).astype(jnp.int32)

    plan = []
    hops = [chips // 2] + [hop for hop in range(1, chips) if hop != chips // 2]
    for hop in hops:
        at = 0
        for piece in PIECES if hop == hops[-1] else (sum(PIECES),):
            plan.append((hop, at * grain, piece * grain))
            at += piece

    def send(index, piece):
        turn = [(p, (p + 2 * plan[index][0]) % groups) for p in range(groups)]
        return lax.ppermute(piece, "pop", turn)

    factor = 1.0 / math.sqrt(depth * rank * count * groups)
    piece, mark = cut(weight, *plan[0][1:], selected)
    arrived = [send(0, piece)]
    packed, left, right, mark = pick(
        factor, selected, shaping, old_left, old_right, width, mark
    )
    packed = send(0, packed)
    piece, mark = cut(weight, *plan[1][1:], mark)
    arrived.append(send(1, piece))
    tall = count * rank
    lefts, rights = unpack(packed, tall, slab, old_right.shape[2])
    left, right = jnp.concatenate([left, lefts], 0), jnp.concatenate([right, rights], 0)
    for bit in bits(chips, 2):
        left = jnp.concatenate([left, swap(left, "pop", bit)], 0)
        right = jnp.concatenate([right, swap(right, "pop", bit)], 0)
    left, mark = gate(left[None], mark)
    sibling = swap(weight, "pop", 1)
    rights = new_right.reshape(members * rank, -1)
    proj = project(tokens, new_left.reshape(-1, slab), rank, each, where, mark)
    piece, mark = cut(weight, *plan[2][1:], mark)
    spare, ready = cut(weight, *plan[3][1:], mark)
    for turns, bit in enumerate(bits(lax.axis_size("col"))):
        left = jnp.concatenate([left, swap(left, "col", bit)], 0)
        if turns == 0:
            arrived[0], mark = gate(arrived[0], left)
            piece, mark = gate(piece, mark)
            arrived.append(send(2, piece))
            right, _ = gate(right, mark)
            right = jnp.concatenate([right, swap(right, "pop", 1)], 0)
            sibling, mark = gate(sibling, mark)
            left, mark = gate(left, mark, proj, ready)
        elif bit * 2 < lax.axis_size("col"):
            left, _ = gate(left, proj)
        else:
            arrived[1], mark = gate(arrived[1], left, proj)
            spare, mark = gate(spare, mark)
            arrived.append(send(3, spare))
            left, _ = gate(left, mark, rights)
        proj = proj + swap(proj, "col", bit)
    left = turn(jnp.concatenate([left, swap(left, "pop", 1)], 1), where)
    spread = spread_out(proj, members, rank, each)

    def run(block, wt, start, before, acts, after, keep=False):
        return run_block(
            jnp.reshape(block, (1,)).astype(jnp.int32),
            tokens, wt, left, right, start, scale, spread, rights, acts, before, after, keep,
        )

    narrow = width % 128 != 0
    core = lax.rem(me, 2)

    def pair(own, other):
        return jnp.where(
            core == 0, jnp.concatenate([own, other], 1), jnp.concatenate([other, own], 1)
        )

    whole = (rows, width * groups)
    if narrow:
        acts, both, done = run(me // 2, pair(weight, sibling), 0, None, whole, where, keep=True)
        updated = lax.dynamic_slice_in_dim(both, core * width, width, 1)
    else:
        acts, updated, done = run(me, weight, 0, None, whole, where, keep=True)
    if not narrow:
        acts, done = run(me ^ 1, sibling, 0, None, acts, done)
    many = [index for index, part in enumerate(plan) if part[0] == hops[-1]][:-2]
    for index, (hop, start, size) in enumerate(plan):
        part = arrived[index]
        if index > 1:
            part, mark = gate(part, done)
            arrived[index] = part
            if index + 2 < len(plan):
                piece, _ = cut(weight, *plan[index + 2][1:], mark)
                arrived.append(send(index + 2, piece))
        if index in many:
            if index != many[-1]:
                continue
            part = jnp.concatenate([arrived[i] for i in many[:-1]] + [part], 0)
            start, size = 0, part.shape[0]
        other = swap(part, "pop", 1)
        if start == 0:
            sums = [None, None]
        ends = start + size == depth
        source = lax.rem(me - 2 * hop + 2 * groups, groups)
        tasks = ((source, part), (source ^ 1, other))
        if narrow:
            tasks = ((source // 2, pair(part, other)),)
        for side, (block, wt) in enumerate(tasks):
            got = run(block, wt, start, sums[side], acts if ends else None, done)
            if not ends:
                sums[side] = done = got
            elif start == 0:
                acts, done = got
            else:
                acts = got
    return updated, acts


def solution(mesh):
    placed = (
        P("pop", None),
        P(None, ("col", "pop")),
        P("pop", None, "col"),
        P("pop", None, "col"),
        P("pop", None),
        P("pop", None),
        P("pop", None, "col"),
        P("pop", None, "col"),
    )
    return jax.shard_map(
        local,
        mesh=mesh,
        in_specs=placed,
        out_specs=(P(None, ("col", "pop")), P("pop", "col")),
        check_vma=False,
    )
```

```python
import functools
import math

import jax
import jax.numpy as jnp
from jax import lax
from jax.experimental import pallas as pl
from jax.experimental.pallas import tpu as pltpu
from jax.sharding import PartitionSpec as P

noise_scale = 0.5
PIECES = (5, 9, 2)
LIMIT = 20 * 2**20
WIDE = 58 * 2**20


def params(limit=LIMIT):
    return pltpu.CompilerParams(dimension_semantics=("arbitrary",), vmem_limit_bytes=limit)


def cost(flops=1, moved=1):
    return pl.CostEstimate(flops=flops, bytes_accessed=moved, transcendentals=0)


def swap(array, axis, bit):
    return lax.ppermute(array, axis, [(i, i ^ bit) for i in range(lax.axis_size(axis))])


def bits(size, least=1):
    bit = least
    while bit < size:
        yield bit
        bit *= 2


MARK = jax.ShapeDtypeStruct((8, 128), jnp.float32)


def vmem():
    return pl.BlockSpec(memory_space=pltpu.VMEM)


def anywhere():
    return pl.BlockSpec(memory_space=pl.ANY)


def gate_kernel(mark_at, *refs):
    refs[mark_at][...] = jnp.zeros(MARK.shape, MARK.dtype)


def gate_all(arrays, *after):
    count = len(arrays)
    return pl.pallas_call(
        functools.partial(gate_kernel, 2 * count + len(after)),
        in_specs=[anywhere()] * (count + len(after)),
        out_specs=[anywhere()] * count + [vmem()],
        out_shape=[jax.ShapeDtypeStruct(array.shape, array.dtype) for array in arrays] + [MARK],
        input_output_aliases={index: index for index in range(count)},
        compiler_params=pltpu.CompilerParams(vmem_limit_bytes=2**20),
        cost_estimate=cost(),
    )(*arrays, *after)


def gate(array, *after):
    return gate_all([array], *after)


def cut_kernel(start, wt, after, out, mark, sem):
    copy = pltpu.make_async_copy(wt.at[pl.ds(start, out.shape[0])], out, sem)
    copy.start()
    copy.wait()
    mark[...] = jnp.zeros(MARK.shape, MARK.dtype)


def cut(weight, start, depth, after):
    return pl.pallas_call(
        functools.partial(cut_kernel, start),
        in_specs=[anywhere()] * 2,
        out_specs=[vmem()] * 2,
        out_shape=[jax.ShapeDtypeStruct((depth, weight.shape[1]), weight.dtype), MARK],
        scratch_shapes=[pltpu.SemaphoreType.DMA],
        compiler_params=pltpu.CompilerParams(vmem_limit_bytes=WIDE - 2 * depth * weight.shape[1]),
        cost_estimate=cost(1, 8 * depth * weight.shape[1]),
    )(weight, after)


def pick_kernel(
    factor, picked, shaping, lefts, rights, after, packed, left, right, mark, some_left, some_right, sems
):
    chosen, width = picked.shape[1], packed.shape[1]
    tall = chosen * lefts.shape[1]
    copies = []
    for slot in range(chosen):
        member = picked[0, slot]
        for source, kept in ((lefts, some_left), (rights, some_right)):
            sem = sems.at[len(copies)]
            copies.append(pltpu.make_async_copy(source.at[member], kept.at[slot], sem))
    for copy in copies:
        copy.start()
    for copy in copies:
        copy.wait()
    scaled, plain = [], []
    for slot in range(chosen):
        scale = shaping[0, slot] * factor
        scaled.append(some_left[slot].astype(jnp.float32) * scale)
        plain.append(some_right[slot].astype(jnp.float32))
    scaled = jnp.concatenate(scaled, 0).astype(jnp.bfloat16)
    plain = jnp.concatenate(plain, 0).astype(jnp.bfloat16)
    left[...] = scaled
    right[...] = plain
    at = 0
    for whole in (scaled, plain):
        for block in range(whole.shape[1] // width):
            packed[at : at + tall, :] = whole[:, block * width : (block + 1) * width]
            at += tall
    mark[...] = jnp.zeros(MARK.shape, MARK.dtype)


def pick(factor, selected, shaping, old_left, old_right, width, after):
    chosen, rank = selected.shape[1], old_left.shape[1]
    tall = chosen * rank
    slab, wide, kind = old_left.shape[2], old_right.shape[2], old_left.dtype
    return pl.pallas_call(
        functools.partial(pick_kernel, factor),
        in_specs=[pl.BlockSpec(memory_space=pltpu.SMEM)] * 2 + [anywhere()] * 3,
        out_specs=[vmem()] * 4,
        out_shape=[
            jax.ShapeDtypeStruct((tall * (slab + wide) // width, width), kind),
            jax.ShapeDtypeStruct((tall, slab), kind),
            jax.ShapeDtypeStruct((tall, wide), kind),
            MARK,
        ],
        scratch_shapes=[
            pltpu.VMEM((chosen, rank, slab), kind),
            pltpu.VMEM((chosen, rank, wide), kind),
            pltpu.SemaphoreType.DMA((2 * chosen,)),
        ],
        compiler_params=pltpu.CompilerParams(vmem_limit_bytes=WIDE),
        cost_estimate=cost(),
    )(selected, shaping, old_left, old_right, after)


def unpack(packed, tall, slab, wide):
    width = packed.shape[1]
    blocks = [slab // width, wide // width]
    got, at = [], 0
    for count in blocks:
        got.append(
            jnp.concatenate([packed[at + tall * i : at + tall * (i + 1)] for i in range(count)], 1)
        )
        at += tall * count
    return got


def mine(shape, rank, each):
    row = lax.broadcasted_iota(jnp.int32, shape, 0)
    token = lax.broadcasted_iota(jnp.int32, shape, 1)
    return lax.div(row, rank) == lax.div(token, each)


def proj_kernel(rank, each, where, left, tok, after, out):
    full = lax.dot_general(
        left[...], tok[...], (((1,), (1,)), ((), ())), preferred_element_type=jnp.float32
    )
    full = jnp.where(mine(full.shape, rank, each), full, 0.0)
    out[...] = full.reshape(-1, *out.shape).sum(0)


def project(tokens, lefts, rank, each, where, after):
    rows, slab = tokens.shape[0], lefts.shape[1]
    return pl.pallas_call(
        functools.partial(proj_kernel, rank, each),
        grid_spec=pltpu.PrefetchScalarGridSpec(
            num_scalar_prefetch=1,
            grid=(1,),
            in_specs=[
                pl.BlockSpec(lefts.shape, lambda k, at: (0, 0)),
                pl.BlockSpec((rows, slab), lambda k, at: (0, at[1])),
                pl.BlockSpec(memory_space=pl.ANY),
            ],
            out_specs=pl.BlockSpec((2 * rank, rows), lambda k, at: (0, 0)),
        ),
        out_shape=jax.ShapeDtypeStruct((2 * rank, rows), jnp.float32),
        compiler_params=params(WIDE),
        cost_estimate=cost(2 * rows * slab * lefts.shape[0], 8 * rows * slab),
    )(where, lefts, tokens, after)


def flipped(index, size):
    got = index * 0
    bit = 1
    while bit < size:
        got = got * 2 + ((index // bit) & 1)
        bit *= 2
    return got


def turn_kernel(where, left, out):
    out[...] = left[...].T


def turn(left, where):
    blocks, sels, slab = left.shape
    return pl.pallas_call(
        turn_kernel,
        grid_spec=pltpu.PrefetchScalarGridSpec(
            num_scalar_prefetch=1,
            grid=(blocks,),
            in_specs=[pl.BlockSpec((None, sels, slab), lambda k, at: (flipped(k ^ at[1], blocks), 0, 0))],
            out_specs=pl.BlockSpec((slab, sels), lambda k, at: (k, 0)),
        ),
        out_shape=jax.ShapeDtypeStruct((blocks * slab, sels), left.dtype),
        compiler_params=params(),
        cost_estimate=cost(),
    )(where, left)


def spread_kernel(rank, each, proj, out):
    narrow = proj[...].astype(jnp.bfloat16).astype(jnp.float32)
    full = jnp.tile(narrow, (out.shape[1] // narrow.shape[0], 1))
    out[...] = jnp.where(mine(full.shape, rank, each), full, 0.0).T.astype(jnp.bfloat16)


def spread_out(proj, members, rank, each):
    return pl.pallas_call(
        functools.partial(spread_kernel, rank, each),
        in_specs=[pl.BlockSpec(memory_space=pltpu.VMEM)],
        out_specs=pl.BlockSpec(memory_space=pltpu.VMEM),
        out_shape=jax.ShapeDtypeStruct((proj.shape[1], members * rank), jnp.bfloat16),
        compiler_params=pltpu.CompilerParams(vmem_limit_bytes=LIMIT),
        cost_estimate=cost(),
    )(proj)


def columns(ref, at, width):
    return ref[:, pl.ds(pl.multiple_of(at * width, width), width)]


def refresh(wt, left, right):
    delta = jnp.dot(left, right, preferred_element_type=jnp.float32)
    return (wt.astype(jnp.float32) + delta).astype(jnp.bfloat16)


def finish(total):
    return (jnp.maximum(total, 0.0) ** 2).astype(jnp.bfloat16)


def begin(scale, spread, rights):
    return scale * jnp.dot(spread, rights, preferred_element_type=jnp.float32)


def full_kernel(scale, keep, begun, where, tok, wt, left, right, spread, rights, *refs):
    out, mark, held = refs[1 if begun else 2], refs[-2], refs[-1]
    step = pl.program_id(0)

    @pl.when(step == 0)
    def _():
        mark[...] = jnp.zeros(MARK.shape, MARK.dtype)
        held[...] = begin(scale, spread[...], rights[...])

    fresh = refresh(wt[...], left[...], right[...])
    if keep:
        refs[-3][...] = fresh
    held[...] += jnp.dot(tok[...], fresh, preferred_element_type=jnp.float32)

    @pl.when(step == pl.num_programs(0) - 1)
    def _():
        out[...] = finish(held[...])


def product(start, where, tok, wt, left, right):
    unit, width = wt.shape
    fresh = refresh(wt[...], left[start : start + unit, :], columns(right, where[0], width))

    def rows(at, size):
        some = tok[at : at + size, start : start + unit]
        return jnp.dot(some, fresh, preferred_element_type=jnp.float32)

    return rows


def sum_kernel(scale, start, where, tok, wt, left, right, *refs):
    out = refs[-1]
    if start == 0:
        before = begin(scale, refs[0][...], columns(refs[1], where[0], wt.shape[1]))
    else:
        before = refs[0][...]
    out[...] = before + product(start, where, tok, wt, left, right)(0, tok.shape[0])


def last_kernel(start, where, tok, wt, left, right, before, acts, out, kept, sems):
    width = wt.shape[1]
    got = product(start, where, tok, wt, left, right)
    part = kept.shape[0] // 2
    place = pl.ds(pl.multiple_of(where[0] * width, width), width)
    copies = []
    for half in range(2):
        rows = pl.ds(half * part, part)
        kept[rows, :] = finish(before[rows, :] + got(half * part, part))
        copies.append(pltpu.make_async_copy(kept.at[rows], out.at[rows, place], sems.at[half]))
        copies[-1].start()
    for copy in copies:
        copy.wait()


def call(
    kernel, where, grid, specs, args, out_specs, out_shape, aliases=None, scratch=(), limit=LIMIT
):
    return pl.pallas_call(
        kernel,
        grid_spec=pltpu.PrefetchScalarGridSpec(
            num_scalar_prefetch=1,
            grid=grid,
            in_specs=specs,
            out_specs=out_specs,
            scratch_shapes=list(scratch),
        ),
        out_shape=out_shape,
        input_output_aliases=aliases or {},
        compiler_params=params(limit),
        cost_estimate=cost(),
    )(where, *args)


def run_block(where, tokens, wt, left, right, start, scale, spread, rights, acts, before, after, keep):
    rows = tokens.shape[0]
    depth, width = wt.shape
    first, last, begun = start == 0, acts is not None, isinstance(acts, tuple)
    tile = pl.BlockSpec((rows, width), lambda k, at: (0, at[0]))
    if first and last:
        unit = depth // 4
        block = pl.BlockSpec((unit, width), lambda k, at: (k, 0))
        specs = [
            pl.BlockSpec((rows, unit), lambda k, at: (0, k)),
            block,
            pl.BlockSpec((unit, left.shape[1]), lambda k, at: (k, 0)),
            pl.BlockSpec((right.shape[0], width), lambda k, at: (0, at[0])),
            pl.BlockSpec(spread.shape, lambda k, at: (0, 0)),
            pl.BlockSpec((rights.shape[0], width), lambda k, at: (0, at[0])),
            anywhere(),
        ]
        args = [tokens, wt, left, right, spread, rights, after]
        aliases = {}
        if not begun:
            specs, args = specs + [anywhere()], args + [acts]
            aliases = {len(args): 0}
        shape = acts if begun else acts.shape
        out_shape, out_specs = [jax.ShapeDtypeStruct(shape, jnp.bfloat16)], [tile]
        if keep:
            out_shape.append(jax.ShapeDtypeStruct((depth, width), jnp.bfloat16))
            out_specs.append(block)
        out_shape.append(MARK)
        out_specs.append(vmem())
        return call(
            functools.partial(full_kernel, scale, keep, begun),
            where, (4,), specs, args, out_specs, out_shape, aliases,
            [pltpu.VMEM((rows, width), jnp.float32)], WIDE,
        )
    if not last:
        extra = [spread, rights] if first else [before]
        return call(
            functools.partial(sum_kernel, scale, start),
            where, (1,), [vmem()] * (4 + len(extra)) + [anywhere()],
            [tokens, wt, left, right, *extra, after], vmem(),
            jax.ShapeDtypeStruct((rows, width), jnp.float32), {} if first else {5: 0},
        )
    return call(
        functools.partial(last_kernel, start),
        where, (1,), [vmem()] * 5 + [anywhere()],
        [tokens, wt, left, right, before, acts], anywhere(),
        jax.ShapeDtypeStruct(acts.shape, jnp.bfloat16), {6: 0},
        [pltpu.VMEM((rows, width), jnp.bfloat16), pltpu.SemaphoreType.DMA((2,))],
    )


def local(tokens, weight, old_left, old_right, selected, shaping, new_left, new_right):
    groups = lax.axis_size("pop")
    me = lax.axis_index("pop")
    spot = lax.axis_index("col")
    depth, width = weight.shape
    members, rank, slab = new_left.shape
    rows = tokens.shape[0]
    each = rows // members
    count = selected.shape[1]
    scale = noise_scale / math.sqrt(depth * rank)
    grain = depth // sum(PIECES)
    chips = groups // 2
    where = jnp.stack([me, spot]).astype(jnp.int32)

    plan = []
    hops = [chips // 2] + [hop for hop in range(1, chips) if hop != chips // 2]
    for hop in hops:
        at = 0
        for piece in PIECES if hop == hops[-1] else (sum(PIECES),):
            plan.append((hop, at * grain, piece * grain))
            at += piece

    def send(index, piece):
        turn = [(p, (p + 2 * plan[index][0]) % groups) for p in range(groups)]
        return lax.ppermute(piece, "pop", turn)

    factor = 1.0 / math.sqrt(depth * rank * count * groups)
    packed, left, right, mark = pick(
        factor, selected, shaping, old_left, old_right, width, selected
    )
    packed = send(0, packed)
    piece, mark = cut(weight, *plan[0][1:], mark)
    arrived = [send(0, piece)]
    tall = count * rank
    sibling, mark = gate(swap(weight, "pop", 1), mark)
    lefts, rights = unpack(packed, tall, slab, old_right.shape[2])
    left, right = jnp.concatenate([left, lefts], 0), jnp.concatenate([right, rights], 0)
    for bit in bits(chips, 2):
        left = jnp.concatenate([left, swap(left, "pop", bit)], 0)
        right = jnp.concatenate([right, swap(right, "pop", bit)], 0)
    left, mark = gate(left[None], mark)
    rights = new_right.reshape(members * rank, -1)
    proj = project(tokens, new_left.reshape(-1, slab), rank, each, where, mark)
    piece, early = cut(weight, *plan[1][1:], mark)
    arrived.append(send(1, piece))
    turns = list(bits(lax.axis_size("col")))[::-1]
    for turn_at, bit in enumerate(turns):
        left = jnp.concatenate([left, swap(left, "col", bit)], 0)
        partial = proj
        proj = proj + swap(proj, "col", bit)
        if turn_at == 0:
            left, right, mark = gate_all([left, right], early, partial)
            right = jnp.concatenate([right, swap(right, "pop", 1)], 0)
            spare, ready = cut(weight, *plan[2][1:], mark)
        elif turn_at < len(turns) - 1:
            left, mark = gate(left, partial)
    left, arrived[0], spare, mark = gate_all([left, arrived[0], spare], partial, rights, ready)
    arrived.append(send(2, spare))
    left = turn(jnp.concatenate([left, swap(left, "pop", 1)], 1), where)
    spread = spread_out(proj, members, rank, each)

    def run(block, wt, start, before, acts, after, keep=False):
        return run_block(
            jnp.reshape(block, (1,)).astype(jnp.int32),
            tokens, wt, left, right, start, scale, spread, rights, acts, before, after, keep,
        )

    narrow = width % 128 != 0
    core = lax.rem(me, 2)

    def pair(own, other):
        return jnp.where(
            core == 0, jnp.concatenate([own, other], 1), jnp.concatenate([other, own], 1)
        )

    whole = (rows, width * groups)
    if narrow:
        acts, both, done = run(me // 2, pair(weight, sibling), 0, None, whole, where, keep=True)
        updated = lax.dynamic_slice_in_dim(both, core * width, width, 1)
    else:
        acts, updated, done = run(me, weight, 0, None, whole, where, keep=True)
    if not narrow:
        acts, done = run(me ^ 1, sibling, 0, None, acts, done)
    many = [index for index, part in enumerate(plan) if part[0] == hops[-1]][:-2]
    for index, (hop, start, size) in enumerate(plan):
        part = arrived[index]
        if index > 0:
            part, mark = gate(part, done)
            arrived[index] = part
            if index + 2 < len(plan):
                piece, _ = cut(weight, *plan[index + 2][1:], mark)
                arrived.append(send(index + 2, piece))
        if index in many:
            if index != many[-1]:
                continue
            part = jnp.concatenate([arrived[i] for i in many[:-1]] + [part], 0)
            start, size = 0, part.shape[0]
        other = swap(part, "pop", 1)
        if start == 0:
            sums = [None, None]
        ends = start + size == depth
        source = lax.rem(me - 2 * hop + 2 * groups, groups)
        tasks = ((source, part), (source ^ 1, other))
        if narrow:
            tasks = ((source // 2, pair(part, other)),)
        for side, (block, wt) in enumerate(tasks):
            got = run(block, wt, start, sums[side], acts if ends else None, done)
            if not ends:
                sums[side] = done = got
            elif start == 0:
                acts, done = got
            else:
                acts = got
    return updated, acts


def solution(mesh):
    placed = (
        P("pop", None),
        P(None, ("col", "pop")),
        P("pop", None, "col"),
        P("pop", None, "col"),
        P("pop", None),
        P("pop", None),
        P("pop", None, "col"),
        P("pop", None, "col"),
    )
    return jax.shard_map(
        local,
        mesh=mesh,
        in_specs=placed,
        out_specs=(P(None, ("col", "pop")), P("pop", "col")),
        check_vma=False,
    )
```

```python
import functools
import math

import jax
import jax.numpy as jnp
from jax import lax
from jax.experimental import pallas as pl
from jax.experimental.pallas import tpu as pltpu
from jax.sharding import PartitionSpec as P

noise_scale = 0.5
PIECES = (1, 5, 9, 1)
LIMIT = 20 * 2**20
WIDE = 58 * 2**20


def params(limit=LIMIT):
    return pltpu.CompilerParams(dimension_semantics=("arbitrary",), vmem_limit_bytes=limit)


def cost(flops=1, moved=1):
    return pl.CostEstimate(flops=flops, bytes_accessed=moved, transcendentals=0)


def swap(array, axis, bit):
    return lax.ppermute(array, axis, [(i, i ^ bit) for i in range(lax.axis_size(axis))])


def bits(size, least=1):
    bit = least
    while bit < size:
        yield bit
        bit *= 2


MARK = jax.ShapeDtypeStruct((8, 128), jnp.float32)


def vmem():
    return pl.BlockSpec(memory_space=pltpu.VMEM)


def anywhere():
    return pl.BlockSpec(memory_space=pl.ANY)


def gate_kernel(mark_at, *refs):
    refs[mark_at][...] = jnp.zeros(MARK.shape, MARK.dtype)


def gate_all(arrays, *after):
    count = len(arrays)
    return pl.pallas_call(
        functools.partial(gate_kernel, 2 * count + len(after)),
        in_specs=[anywhere()] * (count + len(after)),
        out_specs=[anywhere()] * count + [vmem()],
        out_shape=[jax.ShapeDtypeStruct(array.shape, array.dtype) for array in arrays] + [MARK],
        input_output_aliases={index: index for index in range(count)},
        compiler_params=pltpu.CompilerParams(vmem_limit_bytes=2**20),
        cost_estimate=cost(),
    )(*arrays, *after)


def gate(array, *after):
    return gate_all([array], *after)


def cut_kernel(start, wt, after, out, mark, sem):
    copy = pltpu.make_async_copy(wt.at[pl.ds(start, out.shape[0])], out, sem)
    copy.start()
    copy.wait()
    mark[...] = jnp.zeros(MARK.shape, MARK.dtype)


def cut(weight, start, depth, after):
    return pl.pallas_call(
        functools.partial(cut_kernel, start),
        in_specs=[anywhere()] * 2,
        out_specs=[vmem()] * 2,
        out_shape=[jax.ShapeDtypeStruct((depth, weight.shape[1]), weight.dtype), MARK],
        scratch_shapes=[pltpu.SemaphoreType.DMA],
        compiler_params=pltpu.CompilerParams(vmem_limit_bytes=WIDE - 2 * depth * weight.shape[1]),
        cost_estimate=cost(1, 8 * depth * weight.shape[1]),
    )(weight, after)


def pick_kernel(
    factor, picked, shaping, lefts, rights, after, packed, left, right, mark, some_left, some_right, sems
):
    chosen, width = picked.shape[1], packed.shape[1]
    tall = chosen * lefts.shape[1]
    copies = []
    for slot in range(chosen):
        member = picked[0, slot]
        for source, kept in ((lefts, some_left), (rights, some_right)):
            sem = sems.at[len(copies)]
            copies.append(pltpu.make_async_copy(source.at[member], kept.at[slot], sem))
    for copy in copies:
        copy.start()
    for copy in copies:
        copy.wait()
    scaled, plain = [], []
    for slot in range(chosen):
        scale = shaping[0, slot] * factor
        scaled.append(some_left[slot].astype(jnp.float32) * scale)
        plain.append(some_right[slot].astype(jnp.float32))
    scaled = jnp.concatenate(scaled, 0).astype(jnp.bfloat16)
    plain = jnp.concatenate(plain, 0).astype(jnp.bfloat16)
    left[...] = scaled
    right[...] = plain
    at = 0
    for whole in (scaled, plain):
        for block in range(whole.shape[1] // width):
            packed[at : at + tall, :] = whole[:, block * width : (block + 1) * width]
            at += tall
    mark[...] = jnp.zeros(MARK.shape, MARK.dtype)


def pick(factor, selected, shaping, old_left, old_right, width, after):
    chosen, rank = selected.shape[1], old_left.shape[1]
    tall = chosen * rank
    slab, wide, kind = old_left.shape[2], old_right.shape[2], old_left.dtype
    return pl.pallas_call(
        functools.partial(pick_kernel, factor),
        in_specs=[pl.BlockSpec(memory_space=pltpu.SMEM)] * 2 + [anywhere()] * 3,
        out_specs=[vmem()] * 4,
        out_shape=[
            jax.ShapeDtypeStruct((tall * (slab + wide) // width, width), kind),
            jax.ShapeDtypeStruct((tall, slab), kind),
            jax.ShapeDtypeStruct((tall, wide), kind),
            MARK,
        ],
        scratch_shapes=[
            pltpu.VMEM((chosen, rank, slab), kind),
            pltpu.VMEM((chosen, rank, wide), kind),
            pltpu.SemaphoreType.DMA((2 * chosen,)),
        ],
        compiler_params=pltpu.CompilerParams(vmem_limit_bytes=WIDE),
        cost_estimate=cost(),
    )(selected, shaping, old_left, old_right, after)


def unpack(packed, tall, slab, wide):
    width = packed.shape[1]
    blocks = [slab // width, wide // width]
    got, at = [], 0
    for count in blocks:
        got.append(
            jnp.concatenate([packed[at + tall * i : at + tall * (i + 1)] for i in range(count)], 1)
        )
        at += tall * count
    return got


def mine(shape, rank, each):
    row = lax.broadcasted_iota(jnp.int32, shape, 0)
    token = lax.broadcasted_iota(jnp.int32, shape, 1)
    return lax.div(row, rank) == lax.div(token, each)


def proj_kernel(rank, each, where, left, tok, after, out):
    full = lax.dot_general(
        left[...], tok[...], (((1,), (1,)), ((), ())), preferred_element_type=jnp.float32
    )
    full = jnp.where(mine(full.shape, rank, each), full, 0.0)
    out[...] = full.reshape(-1, *out.shape).sum(0)


def project(tokens, lefts, rank, each, where, after):
    rows, slab = tokens.shape[0], lefts.shape[1]
    return pl.pallas_call(
        functools.partial(proj_kernel, rank, each),
        grid_spec=pltpu.PrefetchScalarGridSpec(
            num_scalar_prefetch=1,
            grid=(1,),
            in_specs=[
                pl.BlockSpec(lefts.shape, lambda k, at: (0, 0)),
                pl.BlockSpec((rows, slab), lambda k, at: (0, at[1])),
                pl.BlockSpec(memory_space=pl.ANY),
            ],
            out_specs=pl.BlockSpec((2 * rank, rows), lambda k, at: (0, 0)),
        ),
        out_shape=jax.ShapeDtypeStruct((2 * rank, rows), jnp.float32),
        compiler_params=params(WIDE),
        cost_estimate=cost(2 * rows * slab * lefts.shape[0], 8 * rows * slab),
    )(where, lefts, tokens, after)


def flipped(index, size):
    got = index * 0
    bit = 1
    while bit < size:
        got = got * 2 + ((index // bit) & 1)
        bit *= 2
    return got


def turn_kernel(where, left, out):
    out[...] = left[...].T


def turn(left, where):
    blocks, sels, slab = left.shape
    return pl.pallas_call(
        turn_kernel,
        grid_spec=pltpu.PrefetchScalarGridSpec(
            num_scalar_prefetch=1,
            grid=(blocks,),
            in_specs=[pl.BlockSpec((None, sels, slab), lambda k, at: (flipped(k ^ at[1], blocks), 0, 0))],
            out_specs=pl.BlockSpec((slab, sels), lambda k, at: (k, 0)),
        ),
        out_shape=jax.ShapeDtypeStruct((blocks * slab, sels), left.dtype),
        compiler_params=params(),
        cost_estimate=cost(),
    )(where, left)


def spread_kernel(rank, each, proj, out):
    narrow = proj[...].astype(jnp.bfloat16).astype(jnp.float32)
    full = jnp.tile(narrow, (out.shape[1] // narrow.shape[0], 1))
    out[...] = jnp.where(mine(full.shape, rank, each), full, 0.0).T.astype(jnp.bfloat16)


def spread_out(proj, members, rank, each):
    return pl.pallas_call(
        functools.partial(spread_kernel, rank, each),
        in_specs=[pl.BlockSpec(memory_space=pltpu.VMEM)],
        out_specs=pl.BlockSpec(memory_space=pltpu.VMEM),
        out_shape=jax.ShapeDtypeStruct((proj.shape[1], members * rank), jnp.bfloat16),
        compiler_params=pltpu.CompilerParams(vmem_limit_bytes=LIMIT),
        cost_estimate=cost(),
    )(proj)


def columns(ref, at, width):
    return ref[:, pl.ds(pl.multiple_of(at * width, width), width)]


def refresh(wt, left, right):
    delta = jnp.dot(left, right, preferred_element_type=jnp.float32)
    return (wt.astype(jnp.float32) + delta).astype(jnp.bfloat16)


def finish(total):
    return (jnp.maximum(total, 0.0) ** 2).astype(jnp.bfloat16)


def begin(scale, spread, rights):
    return scale * jnp.dot(spread, rights, preferred_element_type=jnp.float32)


def full_kernel(scale, keep, begun, where, tok, wt, left, right, spread, rights, *refs):
    out, mark, held = refs[1 if begun else 2], refs[-2], refs[-1]
    step = pl.program_id(0)

    @pl.when(step == 0)
    def _():
        mark[...] = jnp.zeros(MARK.shape, MARK.dtype)
        held[...] = begin(scale, spread[...], rights[...])

    fresh = refresh(wt[...], left[...], right[...])
    if keep:
        refs[-3][...] = fresh
    held[...] += jnp.dot(tok[...], fresh, preferred_element_type=jnp.float32)

    @pl.when(step == pl.num_programs(0) - 1)
    def _():
        out[...] = finish(held[...])


def product(start, where, tok, wt, left, right):
    unit, width = wt.shape
    fresh = refresh(wt[...], left[start : start + unit, :], columns(right, where[0], width))

    def rows(at, size):
        some = tok[at : at + size, start : start + unit]
        return jnp.dot(some, fresh, preferred_element_type=jnp.float32)

    return rows


def sum_kernel(scale, start, where, tok, wt, left, right, *refs):
    out = refs[-1]
    if start == 0:
        before = begin(scale, refs[0][...], columns(refs[1], where[0], wt.shape[1]))
    else:
        before = refs[0][...]
    out[...] = before + product(start, where, tok, wt, left, right)(0, tok.shape[0])


def last_kernel(start, where, tok, wt, left, right, before, acts, out, kept, sems):
    width = wt.shape[1]
    got = product(start, where, tok, wt, left, right)
    part = kept.shape[0] // 2
    place = pl.ds(pl.multiple_of(where[0] * width, width), width)
    copies = []
    for half in range(2):
        rows = pl.ds(half * part, part)
        kept[rows, :] = finish(before[rows, :] + got(half * part, part))
        copies.append(pltpu.make_async_copy(kept.at[rows], out.at[rows, place], sems.at[half]))
        copies[-1].start()
    for copy in copies:
        copy.wait()


def call(
    kernel, where, grid, specs, args, out_specs, out_shape, aliases=None, scratch=(), limit=LIMIT
):
    return pl.pallas_call(
        kernel,
        grid_spec=pltpu.PrefetchScalarGridSpec(
            num_scalar_prefetch=1,
            grid=grid,
            in_specs=specs,
            out_specs=out_specs,
            scratch_shapes=list(scratch),
        ),
        out_shape=out_shape,
        input_output_aliases=aliases or {},
        compiler_params=params(limit),
        cost_estimate=cost(),
    )(where, *args)


def run_block(where, tokens, wt, left, right, start, scale, spread, rights, acts, before, after, keep):
    rows = tokens.shape[0]
    depth, width = wt.shape
    first, last, begun = start == 0, acts is not None, isinstance(acts, tuple)
    tile = pl.BlockSpec((rows, width), lambda k, at: (0, at[0]))
    if first and last:
        unit = depth // 4
        block = pl.BlockSpec((unit, width), lambda k, at: (k, 0))
        specs = [
            pl.BlockSpec((rows, unit), lambda k, at: (0, k)),
            block,
            pl.BlockSpec((unit, left.shape[1]), lambda k, at: (k, 0)),
            pl.BlockSpec((right.shape[0], width), lambda k, at: (0, at[0])),
            pl.BlockSpec(spread.shape, lambda k, at: (0, 0)),
            pl.BlockSpec((rights.shape[0], width), lambda k, at: (0, at[0])),
            anywhere(),
        ]
        args = [tokens, wt, left, right, spread, rights, after]
        aliases = {}
        if not begun:
            specs, args = specs + [anywhere()], args + [acts]
            aliases = {len(args): 0}
        shape = acts if begun else acts.shape
        out_shape, out_specs = [jax.ShapeDtypeStruct(shape, jnp.bfloat16)], [tile]
        if keep:
            out_shape.append(jax.ShapeDtypeStruct((depth, width), jnp.bfloat16))
            out_specs.append(block)
        out_shape.append(MARK)
        out_specs.append(vmem())
        return call(
            functools.partial(full_kernel, scale, keep, begun),
            where, (4,), specs, args, out_specs, out_shape, aliases,
            [pltpu.VMEM((rows, width), jnp.float32)], WIDE,
        )
    if not last:
        extra = [spread, rights] if first else [before]
        return call(
            functools.partial(sum_kernel, scale, start),
            where, (1,), [vmem()] * (4 + len(extra)) + [anywhere()],
            [tokens, wt, left, right, *extra, after], vmem(),
            jax.ShapeDtypeStruct((rows, width), jnp.float32), {} if first else {5: 0},
        )
    return call(
        functools.partial(last_kernel, start),
        where, (1,), [vmem()] * 5 + [anywhere()],
        [tokens, wt, left, right, before, acts], anywhere(),
        jax.ShapeDtypeStruct(acts.shape, jnp.bfloat16), {6: 0},
        [pltpu.VMEM((rows, width), jnp.bfloat16), pltpu.SemaphoreType.DMA((2,))],
    )


def local(tokens, weight, old_left, old_right, selected, shaping, new_left, new_right):
    groups = lax.axis_size("pop")
    me = lax.axis_index("pop")
    spot = lax.axis_index("col")
    depth, width = weight.shape
    members, rank, slab = new_left.shape
    rows = tokens.shape[0]
    each = rows // members
    count = selected.shape[1]
    scale = noise_scale / math.sqrt(depth * rank)
    grain = depth // sum(PIECES)
    chips = groups // 2
    where = jnp.stack([me, spot]).astype(jnp.int32)

    plan = []
    hops = [chips // 2] + [hop for hop in range(1, chips) if hop != chips // 2]
    for hop in hops:
        at = 0
        for piece in PIECES if hop == hops[-1] else (sum(PIECES),):
            plan.append((hop, at * grain, piece * grain))
            at += piece

    def send(index, piece):
        turn = [(p, (p + 2 * plan[index][0]) % groups) for p in range(groups)]
        return lax.ppermute(piece, "pop", turn)

    factor = 1.0 / math.sqrt(depth * rank * count * groups)
    arrived = [send(0, weight[: plan[0][2]])]
    packed, left, right, mark = pick(
        factor, selected, shaping, old_left, old_right, width, selected
    )
    packed = send(0, packed)
    piece, mark = cut(weight, *plan[1][1:], mark)
    arrived.append(send(1, piece))
    tall = count * rank
    sibling, mark = gate(swap(weight, "pop", 1), mark)
    arrived[0], mark = gate(arrived[0], mark)
    packed, mark = gate(packed, mark)
    lefts, rights = unpack(packed, tall, slab, old_right.shape[2])
    left, right = jnp.concatenate([left, lefts], 0), jnp.concatenate([right, rights], 0)
    for bit in bits(chips, 2):
        left = jnp.concatenate([left, swap(left, "pop", bit)], 0)
        right = jnp.concatenate([right, swap(right, "pop", bit)], 0)
    left, mark = gate(left[None], mark)
    rights = new_right.reshape(members * rank, -1)
    proj = project(tokens, new_left.reshape(-1, slab), rank, each, where, mark)
    turns = list(bits(lax.axis_size("col")))[::-1]
    for turn_at, bit in enumerate(turns):
        left = jnp.concatenate([left, swap(left, "col", bit)], 0)
        partial = proj
        proj = proj + swap(proj, "col", bit)
        if turn_at == 0:
            left, right, mark = gate_all([left, right], partial)
            right = jnp.concatenate([right, swap(right, "pop", 1)], 0)
            piece, early = cut(weight, *plan[2][1:], mark)
            arrived.append(send(2, piece))
        elif turn_at == 1:
            left, mark = gate(left, partial, early, rights)
            spare, ready = cut(weight, *plan[3][1:], mark)
    left, arrived[1], spare, mark = gate_all([left, arrived[1], spare], partial, ready)
    arrived.append(send(3, spare))
    left = turn(jnp.concatenate([left, swap(left, "pop", 1)], 1), where)
    spread = spread_out(proj, members, rank, each)

    def run(block, wt, start, before, acts, after, keep=False):
        return run_block(
            jnp.reshape(block, (1,)).astype(jnp.int32),
            tokens, wt, left, right, start, scale, spread, rights, acts, before, after, keep,
        )

    narrow = width % 128 != 0
    core = lax.rem(me, 2)

    def pair(own, other):
        return jnp.where(
            core == 0, jnp.concatenate([own, other], 1), jnp.concatenate([other, own], 1)
        )

    whole = (rows, width * groups)
    if narrow:
        acts, both, done = run(me // 2, pair(weight, sibling), 0, None, whole, where, keep=True)
        updated = lax.dynamic_slice_in_dim(both, core * width, width, 1)
    else:
        acts, updated, done = run(me, weight, 0, None, whole, where, keep=True)
    if not narrow:
        acts, done = run(me ^ 1, sibling, 0, None, acts, done)
    many = [index for index, part in enumerate(plan) if part[0] == hops[-1]][:-2]
    for index, (hop, start, size) in enumerate(plan):
        part = arrived[index]
        if index > 1:
            part, mark = gate(part, done)
            arrived[index] = part
            if index + 2 < len(plan):
                piece, _ = cut(weight, *plan[index + 2][1:], mark)
                arrived.append(send(index + 2, piece))
        if index in many:
            if index != many[-1]:
                continue
            part = jnp.concatenate([arrived[i] for i in many[:-1]] + [part], 0)
            start, size = 0, part.shape[0]
        other = swap(part, "pop", 1)
        if start == 0:
            sums = [None, None]
        ends = start + size == depth
        source = lax.rem(me - 2 * hop + 2 * groups, groups)
        tasks = ((source, part), (source ^ 1, other))
        if narrow:
            tasks = ((source // 2, pair(part, other)),)
        for side, (block, wt) in enumerate(tasks):
            got = run(block, wt, start, sums[side], acts if ends else None, done)
            if not ends:
                sums[side] = done = got
            elif start == 0:
                acts, done = got
            else:
                acts = got
    return updated, acts


def solution(mesh):
    placed = (
        P("pop", None),
        P(None, ("col", "pop")),
        P("pop", None, "col"),
        P("pop", None, "col"),
        P("pop", None),
        P("pop", None),
        P("pop", None, "col"),
        P("pop", None, "col"),
    )
    return jax.shard_map(
        local,
        mesh=mesh,
        in_specs=placed,
        out_specs=(P(None, ("col", "pop")), P("pop", "col")),
        check_vma=False,
    )
```

```python
import functools
import math

import jax
import jax.numpy as jnp
from jax import lax
from jax.experimental import pallas as pl
from jax.experimental.pallas import tpu as pltpu
from jax.sharding import PartitionSpec as P

noise_scale = 0.5
PIECES = (1, 5, 9, 1)
LIMIT = 20 * 2**20
WIDE = 58 * 2**20
BROAD = 50 * 2**20


def params(limit=LIMIT):
    return pltpu.CompilerParams(dimension_semantics=("arbitrary",), vmem_limit_bytes=limit)


def cost(flops=1, moved=1):
    return pl.CostEstimate(flops=flops, bytes_accessed=moved, transcendentals=0)


def swap(array, axis, bit):
    return lax.ppermute(array, axis, [(i, i ^ bit) for i in range(lax.axis_size(axis))])


def bits(size, least=1):
    bit = least
    while bit < size:
        yield bit
        bit *= 2


MARK = jax.ShapeDtypeStruct((8, 128), jnp.float32)


def vmem():
    return pl.BlockSpec(memory_space=pltpu.VMEM)


def anywhere():
    return pl.BlockSpec(memory_space=pl.ANY)


def gate_kernel(mark_at, *refs):
    refs[mark_at][...] = jnp.zeros(MARK.shape, MARK.dtype)


def gate_all(arrays, *after):
    count = len(arrays)
    return pl.pallas_call(
        functools.partial(gate_kernel, 2 * count + len(after)),
        in_specs=[anywhere()] * (count + len(after)),
        out_specs=[anywhere()] * count + [vmem()],
        out_shape=[jax.ShapeDtypeStruct(array.shape, array.dtype) for array in arrays] + [MARK],
        input_output_aliases={index: index for index in range(count)},
        compiler_params=pltpu.CompilerParams(vmem_limit_bytes=2**20),
        cost_estimate=cost(),
    )(*arrays, *after)


def gate(array, *after):
    return gate_all([array], *after)


def hold_kernel(*refs):
    pass


def hold(array, *after):
    return pl.pallas_call(
        hold_kernel,
        in_specs=[anywhere()] * (1 + len(after)),
        out_specs=anywhere(),
        out_shape=jax.ShapeDtypeStruct(array.shape, array.dtype),
        input_output_aliases={0: 0},
        compiler_params=pltpu.CompilerParams(vmem_limit_bytes=2**20),
        cost_estimate=cost(),
    )(array, *after)


def cut_kernel(start, wt, after, out, mark, sem):
    copy = pltpu.make_async_copy(wt.at[pl.ds(start, out.shape[0])], out, sem)
    copy.start()
    copy.wait()
    mark[...] = jnp.zeros(MARK.shape, MARK.dtype)


def cut(weight, start, depth, after):
    return pl.pallas_call(
        functools.partial(cut_kernel, start),
        in_specs=[anywhere()] * 2,
        out_specs=[vmem()] * 2,
        out_shape=[jax.ShapeDtypeStruct((depth, weight.shape[1]), weight.dtype), MARK],
        scratch_shapes=[pltpu.SemaphoreType.DMA],
        compiler_params=pltpu.CompilerParams(vmem_limit_bytes=WIDE - 2 * depth * weight.shape[1]),
        cost_estimate=cost(1, 8 * depth * weight.shape[1]),
    )(weight, after)


def pick_kernel(
    factor, picked, shaping, lefts, rights, after, packed, left, right, mark, some_left, some_right, sems
):
    chosen, width = picked.shape[1], packed.shape[1]
    tall = chosen * lefts.shape[1]
    copies = []
    for slot in range(chosen):
        member = picked[0, slot]
        for source, kept in ((lefts, some_left), (rights, some_right)):
            sem = sems.at[len(copies)]
            copies.append(pltpu.make_async_copy(source.at[member], kept.at[slot], sem))
    for copy in copies:
        copy.start()
    for copy in copies:
        copy.wait()
    scaled, plain = [], []
    for slot in range(chosen):
        scale = shaping[0, slot] * factor
        scaled.append(some_left[slot].astype(jnp.float32) * scale)
        plain.append(some_right[slot].astype(jnp.float32))
    scaled = jnp.concatenate(scaled, 0).astype(jnp.bfloat16)
    plain = jnp.concatenate(plain, 0).astype(jnp.bfloat16)
    left[...] = scaled
    right[...] = plain
    at = 0
    for whole in (scaled, plain):
        for block in range(whole.shape[1] // width):
            packed[at : at + tall, :] = whole[:, block * width : (block + 1) * width]
            at += tall
    mark[...] = jnp.zeros(MARK.shape, MARK.dtype)


def pick(factor, selected, shaping, old_left, old_right, width, after):
    chosen, rank = selected.shape[1], old_left.shape[1]
    tall = chosen * rank
    slab, wide, kind = old_left.shape[2], old_right.shape[2], old_left.dtype
    return pl.pallas_call(
        functools.partial(pick_kernel, factor),
        in_specs=[pl.BlockSpec(memory_space=pltpu.SMEM)] * 2 + [anywhere()] * 3,
        out_specs=[vmem()] * 4,
        out_shape=[
            jax.ShapeDtypeStruct((tall * (slab + wide) // width, width), kind),
            jax.ShapeDtypeStruct((tall, slab), kind),
            jax.ShapeDtypeStruct((tall, wide), kind),
            MARK,
        ],
        scratch_shapes=[
            pltpu.VMEM((chosen, rank, slab), kind),
            pltpu.VMEM((chosen, rank, wide), kind),
            pltpu.SemaphoreType.DMA((2 * chosen,)),
        ],
        compiler_params=pltpu.CompilerParams(vmem_limit_bytes=WIDE),
        cost_estimate=cost(),
    )(selected, shaping, old_left, old_right, after)


def unpack(packed, tall, slab, wide):
    width = packed.shape[1]
    blocks = [slab // width, wide // width]
    got, at = [], 0
    for count in blocks:
        got.append(
            jnp.concatenate([packed[at + tall * i : at + tall * (i + 1)] for i in range(count)], 1)
        )
        at += tall * count
    return got


def mine(shape, rank, each):
    row = lax.broadcasted_iota(jnp.int32, shape, 0)
    token = lax.broadcasted_iota(jnp.int32, shape, 1)
    return lax.div(row, rank) == lax.div(token, each)


def proj_kernel(rank, each, where, left, tok, after, out):
    full = lax.dot_general(
        left[...], tok[...], (((1,), (1,)), ((), ())), preferred_element_type=jnp.float32
    )
    full = jnp.where(mine(full.shape, rank, each), full, 0.0)
    out[...] = full.reshape(-1, *out.shape).sum(0)


def project(tokens, lefts, rank, each, where, after):
    rows, slab = tokens.shape[0], lefts.shape[1]
    return pl.pallas_call(
        functools.partial(proj_kernel, rank, each),
        grid_spec=pltpu.PrefetchScalarGridSpec(
            num_scalar_prefetch=1,
            grid=(1,),
            in_specs=[
                pl.BlockSpec(lefts.shape, lambda k, at: (0, 0)),
                pl.BlockSpec((rows, slab), lambda k, at: (0, at[1])),
                pl.BlockSpec(memory_space=pl.ANY),
            ],
            out_specs=pl.BlockSpec((2 * rank, rows), lambda k, at: (0, 0)),
        ),
        out_shape=jax.ShapeDtypeStruct((2 * rank, rows), jnp.float32),
        compiler_params=params(WIDE),
        cost_estimate=cost(2 * rows * slab * lefts.shape[0], 8 * rows * slab),
    )(where, lefts, tokens, after)


def flipped(index, size):
    got = index * 0
    bit = 1
    while bit < size:
        got = got * 2 + ((index // bit) & 1)
        bit *= 2
    return got


def turn_kernel(where, left, out):
    out[...] = left[...].T


def turn(left, where):
    blocks, sels, slab = left.shape
    return pl.pallas_call(
        turn_kernel,
        grid_spec=pltpu.PrefetchScalarGridSpec(
            num_scalar_prefetch=1,
            grid=(blocks,),
            in_specs=[pl.BlockSpec((None, sels, slab), lambda k, at: (flipped(k ^ at[1], blocks), 0, 0))],
            out_specs=pl.BlockSpec((slab, sels), lambda k, at: (k, 0)),
        ),
        out_shape=jax.ShapeDtypeStruct((blocks * slab, sels), left.dtype),
        compiler_params=params(),
        cost_estimate=cost(),
    )(where, left)


def spread_kernel(rank, each, proj, out):
    narrow = proj[...].astype(jnp.bfloat16).astype(jnp.float32)
    full = jnp.tile(narrow, (out.shape[1] // narrow.shape[0], 1))
    out[...] = jnp.where(mine(full.shape, rank, each), full, 0.0).T.astype(jnp.bfloat16)


def spread_out(proj, members, rank, each):
    return pl.pallas_call(
        functools.partial(spread_kernel, rank, each),
        in_specs=[pl.BlockSpec(memory_space=pltpu.VMEM)],
        out_specs=pl.BlockSpec(memory_space=pltpu.VMEM),
        out_shape=jax.ShapeDtypeStruct((proj.shape[1], members * rank), jnp.bfloat16),
        compiler_params=pltpu.CompilerParams(vmem_limit_bytes=LIMIT),
        cost_estimate=cost(),
    )(proj)


def columns(ref, at, width):
    return ref[:, pl.ds(pl.multiple_of(at * width, width), width)]


def refresh(wt, left, right):
    delta = jnp.dot(left, right, preferred_element_type=jnp.float32)
    return (wt.astype(jnp.float32) + delta).astype(jnp.bfloat16)


def finish(total):
    return (jnp.maximum(total, 0.0) ** 2).astype(jnp.bfloat16)


def begin(scale, spread, rights):
    return scale * jnp.dot(spread, rights, preferred_element_type=jnp.float32)


def full_kernel(scale, keep, begun, where, tok, wt, left, right, spread, rights, *refs):
    out, mark, held = refs[1 if begun else 2], refs[-2], refs[-1]
    step = pl.program_id(0)

    @pl.when(step == 0)
    def _():
        mark[...] = jnp.zeros(MARK.shape, MARK.dtype)
        held[...] = begin(scale, spread[...], rights[...])

    fresh = refresh(wt[...], left[...], right[...])
    if keep:
        refs[-3][...] = fresh
    held[...] += jnp.dot(tok[...], fresh, preferred_element_type=jnp.float32)

    @pl.when(step == pl.num_programs(0) - 1)
    def _():
        out[...] = finish(held[...])


def product(start, where, tok, wt, left, right):
    unit, width = wt.shape
    fresh = refresh(wt[...], left[start : start + unit, :], columns(right, where[0], width))

    def rows(at, size):
        some = tok[at : at + size, start : start + unit]
        return jnp.dot(some, fresh, preferred_element_type=jnp.float32)

    return rows


def sum_kernel(scale, start, where, tok, wt, left, right, *refs):
    out = refs[-1]
    unit, width = wt.shape
    step = pl.program_id(0)

    @pl.when(step == 0)
    def _():
        if start == 0:
            out[...] = begin(scale, refs[0][...], columns(refs[1], where[0], width))
        else:
            out[...] = refs[0][...]

    at = pl.multiple_of(start + step * unit, 128)
    fresh = refresh(wt[...], left[pl.ds(at, unit), :], columns(right, where[0], width))
    out[...] += jnp.dot(tok[:, pl.ds(at, unit)], fresh, preferred_element_type=jnp.float32)


def last_kernel(start, where, tok, wt, left, right, before, acts, out, kept, sems):
    width = wt.shape[1]
    got = product(start, where, tok, wt, left, right)
    part = kept.shape[0] // 4
    place = pl.ds(pl.multiple_of(where[0] * width, width), width)
    copies = []
    for half in range(4):
        rows = pl.ds(half * part, part)
        kept[rows, :] = finish(before[rows, :] + got(half * part, part))
        copies.append(pltpu.make_async_copy(kept.at[rows], out.at[rows, place], sems.at[half]))
        copies[-1].start()
    for copy in copies:
        copy.wait()


def call(
    kernel, where, grid, specs, args, out_specs, out_shape, aliases=None, scratch=(), limit=LIMIT
):
    return pl.pallas_call(
        kernel,
        grid_spec=pltpu.PrefetchScalarGridSpec(
            num_scalar_prefetch=1,
            grid=grid,
            in_specs=specs,
            out_specs=out_specs,
            scratch_shapes=list(scratch),
        ),
        out_shape=out_shape,
        input_output_aliases=aliases or {},
        compiler_params=params(limit),
        cost_estimate=cost(),
    )(where, *args)


def run_block(where, tokens, wt, left, right, start, scale, spread, rights, acts, before, after, keep):
    rows = tokens.shape[0]
    depth, width = wt.shape
    first, last, begun = start == 0, acts is not None, isinstance(acts, tuple)
    tile = pl.BlockSpec((rows, width), lambda k, at: (0, at[0]))
    if first and last:
        unit = depth // 4
        block = pl.BlockSpec((unit, width), lambda k, at: (k, 0))
        specs = [
            pl.BlockSpec((rows, unit), lambda k, at: (0, k)),
            block,
            pl.BlockSpec((unit, left.shape[1]), lambda k, at: (k, 0)),
            pl.BlockSpec((right.shape[0], width), lambda k, at: (0, at[0])),
            pl.BlockSpec(spread.shape, lambda k, at: (0, 0)),
            pl.BlockSpec((rights.shape[0], width), lambda k, at: (0, at[0])),
            anywhere(),
        ]
        args = [tokens, wt, left, right, spread, rights, after]
        aliases = {}
        if not begun:
            specs, args = specs + [anywhere()], args + [acts]
            aliases = {len(args): 0}
        shape = acts if begun else acts.shape
        out_shape, out_specs = [jax.ShapeDtypeStruct(shape, jnp.bfloat16)], [tile]
        if keep:
            out_shape.append(jax.ShapeDtypeStruct((depth, width), jnp.bfloat16))
            out_specs.append(block)
        out_shape.append(MARK)
        out_specs.append(vmem())
        return call(
            functools.partial(full_kernel, scale, keep, begun),
            where, (4,), specs, args, out_specs, out_shape, aliases,
            [pltpu.VMEM((rows, width), jnp.float32)], BROAD,
        )
    if not last:
        extra = [spread, rights] if first else [before]
        unit = depth
        return call(
            functools.partial(sum_kernel, scale, start),
            where, (depth // unit,),
            [vmem(), pl.BlockSpec((unit, width), lambda k, at: (k, 0))]
            + [vmem()] * (2 + len(extra)) + [anywhere()],
            [tokens, wt, left, right, *extra, after], vmem(),
            jax.ShapeDtypeStruct((rows, width), jnp.float32), {} if first else {5: 0},
        )
    return call(
        functools.partial(last_kernel, start),
        where, (1,), [vmem()] * 5 + [anywhere()],
        [tokens, wt, left, right, before, acts], anywhere(),
        jax.ShapeDtypeStruct(acts.shape, jnp.bfloat16), {6: 0},
        [pltpu.VMEM((rows, width), jnp.bfloat16), pltpu.SemaphoreType.DMA((4,))],
    )


def local(tokens, weight, old_left, old_right, selected, shaping, new_left, new_right):
    groups = lax.axis_size("pop")
    me = lax.axis_index("pop")
    spot = lax.axis_index("col")
    depth, width = weight.shape
    members, rank, slab = new_left.shape
    rows = tokens.shape[0]
    each = rows // members
    count = selected.shape[1]
    scale = noise_scale / math.sqrt(depth * rank)
    grain = depth // sum(PIECES)
    chips = groups // 2
    where = jnp.stack([me, spot]).astype(jnp.int32)

    plan = []
    hops = [chips // 2] + [hop for hop in range(1, chips) if hop != chips // 2]
    for hop in hops:
        at = 0
        for piece in PIECES if hop == hops[-1] else (sum(PIECES),):
            plan.append((hop, at * grain, piece * grain))
            at += piece

    def send(index, piece):
        turn = [(p, (p + 2 * plan[index][0]) % groups) for p in range(groups)]
        return lax.ppermute(piece, "pop", turn)

    factor = 1.0 / math.sqrt(depth * rank * count * groups)
    arrived = [send(0, weight[: plan[0][2]])]
    packed, left, right, mark = pick(
        factor, selected, shaping, old_left, old_right, width, selected
    )
    packed = send(0, packed)
    piece, mark = cut(weight, *plan[1][1:], mark)
    arrived.append(send(1, piece))
    tall = count * rank
    sibling, mark = gate(swap(weight, "pop", 1), mark)
    arrived[0], mark = gate(arrived[0], mark)
    packed, mark = gate(packed, mark)
    lefts, rights = unpack(packed, tall, slab, old_right.shape[2])
    left, right = jnp.concatenate([left, lefts], 0), jnp.concatenate([right, rights], 0)
    for bit in bits(chips, 2):
        left = jnp.concatenate([left, swap(left, "pop", bit)], 0)
        right = jnp.concatenate([right, swap(right, "pop", bit)], 0)
    left, mark = gate(left[None], mark)
    rights = new_right.reshape(members * rank, -1)
    proj = project(tokens, new_left.reshape(-1, slab), rank, each, where, mark)
    turns = list(bits(lax.axis_size("col")))[::-1]
    for turn_at, bit in enumerate(turns):
        left = jnp.concatenate([left, swap(left, "col", bit)], 0)
        partial = proj
        proj = proj + swap(proj, "col", bit)
        if turn_at == 0:
            left, right, mark = gate_all([left, right], partial)
            right = jnp.concatenate([right, swap(right, "pop", 1)], 0)
            piece, early = cut(weight, *plan[2][1:], mark)
            arrived.append(send(2, piece))
        elif turn_at == 1:
            left, mark = gate(left, partial, early, rights)
            spare, ready = cut(weight, *plan[3][1:], mark)
    left, arrived[1], spare, mark = gate_all([left, arrived[1], spare], partial, ready)
    arrived.append(send(3, spare))
    left = turn(jnp.concatenate([left, swap(left, "pop", 1)], 1), where)
    spread = spread_out(proj, members, rank, each)

    def run(block, wt, start, before, acts, after, keep=False):
        return run_block(
            jnp.reshape(block, (1,)).astype(jnp.int32),
            tokens, wt, left, right, start, scale, spread, rights, acts, before, after, keep,
        )

    narrow = width % 128 != 0
    core = lax.rem(me, 2)

    def pair(own, other):
        return jnp.where(
            core == 0, jnp.concatenate([own, other], 1), jnp.concatenate([other, own], 1)
        )

    whole = (rows, width * groups)
    if narrow:
        acts, both, done = run(me // 2, pair(weight, sibling), 0, None, whole, where, keep=True)
        updated = lax.dynamic_slice_in_dim(both, core * width, width, 1)
    else:
        acts, updated, done = run(me, weight, 0, None, whole, where, keep=True)
    if not narrow:
        acts, done = run(me ^ 1, sibling, 0, None, acts, done)
    many = [index for index, part in enumerate(plan) if part[0] == hops[-1]][:-2]
    for index, (hop, start, size) in enumerate(plan):
        part = arrived[index]
        if index > 1:
            part = hold(part, done)
            arrived[index] = part
            if index + 2 < len(plan):
                part, mark = gate(part, done)
                piece, _ = cut(weight, *plan[index + 2][1:], mark)
                arrived.append(send(index + 2, piece))
        if index in many:
            if index != many[-1]:
                continue
            part = jnp.concatenate([arrived[i] for i in many[:-1]] + [part], 0)
            start, size = 0, part.shape[0]
        other = swap(part, "pop", 1)
        if start == 0:
            sums = [None, None]
        ends = start + size == depth
        source = lax.rem(me - 2 * hop + 2 * groups, groups)
        tasks = ((source, part), (source ^ 1, other))
        if narrow:
            tasks = ((source // 2, pair(part, other)),)
        for side, (block, wt) in enumerate(tasks):
            got = run(block, wt, start, sums[side], acts if ends else None, done)
            if not ends:
                sums[side] = done = got
            elif start == 0:
                acts, done = got
            else:
                acts = got
    return updated, acts


def solution(mesh):
    placed = (
        P("pop", None),
        P(None, ("col", "pop")),
        P("pop", None, "col"),
        P("pop", None, "col"),
        P("pop", None),
        P("pop", None),
        P("pop", None, "col"),
        P("pop", None, "col"),
    )
    return jax.shard_map(
        local,
        mesh=mesh,
        in_specs=placed,
        out_specs=(P(None, ("col", "pop")), P("pop", "col")),
        check_vma=False,
    )
```

```python
import functools
import math

import jax
import jax.numpy as jnp
from jax import lax
from jax.experimental import pallas as pl
from jax.experimental.pallas import tpu as pltpu
from jax.sharding import PartitionSpec as P

noise_scale = 0.5
PIECES = (1, 5, 9, 1)
LIMIT = 20 * 2**20
WIDE = 58 * 2**20
BROAD = 50 * 2**20


def params(limit=LIMIT):
    return pltpu.CompilerParams(dimension_semantics=("arbitrary",), vmem_limit_bytes=limit)


def cost(flops=1, moved=1):
    return pl.CostEstimate(flops=flops, bytes_accessed=moved, transcendentals=0)


def swap(array, axis, bit):
    return lax.ppermute(array, axis, [(i, i ^ bit) for i in range(lax.axis_size(axis))])


def bits(size, least=1):
    bit = least
    while bit < size:
        yield bit
        bit *= 2


MARK = jax.ShapeDtypeStruct((8, 128), jnp.float32)


def vmem():
    return pl.BlockSpec(memory_space=pltpu.VMEM)


def anywhere():
    return pl.BlockSpec(memory_space=pl.ANY)


def gate_kernel(mark_at, *refs):
    refs[mark_at][...] = jnp.zeros(MARK.shape, MARK.dtype)


def gate_all(arrays, *after):
    count = len(arrays)
    return pl.pallas_call(
        functools.partial(gate_kernel, 2 * count + len(after)),
        in_specs=[anywhere()] * (count + len(after)),
        out_specs=[anywhere()] * count + [vmem()],
        out_shape=[jax.ShapeDtypeStruct(array.shape, array.dtype) for array in arrays] + [MARK],
        input_output_aliases={index: index for index in range(count)},
        compiler_params=pltpu.CompilerParams(vmem_limit_bytes=2**20),
        cost_estimate=cost(),
    )(*arrays, *after)


def gate(array, *after):
    return gate_all([array], *after)


def hold_kernel(*refs):
    pass


def hold(array, *after):
    return pl.pallas_call(
        hold_kernel,
        in_specs=[anywhere()] * (1 + len(after)),
        out_specs=anywhere(),
        out_shape=jax.ShapeDtypeStruct(array.shape, array.dtype),
        input_output_aliases={0: 0},
        compiler_params=pltpu.CompilerParams(vmem_limit_bytes=2**20),
        cost_estimate=cost(),
    )(array, *after)


def cut_kernel(start, wt, after, out, mark, sem):
    copy = pltpu.make_async_copy(wt.at[pl.ds(start, out.shape[0])], out, sem)
    copy.start()
    copy.wait()
    mark[...] = jnp.zeros(MARK.shape, MARK.dtype)


def cut(weight, start, depth, after):
    return pl.pallas_call(
        functools.partial(cut_kernel, start),
        in_specs=[anywhere()] * 2,
        out_specs=[vmem()] * 2,
        out_shape=[jax.ShapeDtypeStruct((depth, weight.shape[1]), weight.dtype), MARK],
        scratch_shapes=[pltpu.SemaphoreType.DMA],
        compiler_params=pltpu.CompilerParams(vmem_limit_bytes=WIDE - 2 * depth * weight.shape[1]),
        cost_estimate=cost(1, 8 * depth * weight.shape[1]),
    )(weight, after)


def pick_kernel(
    factor, picked, shaping, lefts, rights, after, packed, left, right, mark, some_left, some_right, sems
):
    chosen, width = picked.shape[1], packed.shape[1]
    tall = chosen * lefts.shape[1]
    copies = []
    for slot in range(chosen):
        member = picked[0, slot]
        for source, kept in ((lefts, some_left), (rights, some_right)):
            sem = sems.at[len(copies)]
            copies.append(pltpu.make_async_copy(source.at[member], kept.at[slot], sem))
    for copy in copies:
        copy.start()
    for copy in copies:
        copy.wait()
    scaled, plain = [], []
    for slot in range(chosen):
        scale = shaping[0, slot] * factor
        scaled.append(some_left[slot].astype(jnp.float32) * scale)
        plain.append(some_right[slot].astype(jnp.float32))
    scaled = jnp.concatenate(scaled, 0).astype(jnp.bfloat16)
    plain = jnp.concatenate(plain, 0).astype(jnp.bfloat16)
    left[...] = scaled
    right[...] = plain
    at = 0
    for whole in (scaled, plain):
        for block in range(whole.shape[1] // width):
            packed[at : at + tall, :] = whole[:, block * width : (block + 1) * width]
            at += tall
    mark[...] = jnp.zeros(MARK.shape, MARK.dtype)


def pick(factor, selected, shaping, old_left, old_right, width, after):
    chosen, rank = selected.shape[1], old_left.shape[1]
    tall = chosen * rank
    slab, wide, kind = old_left.shape[2], old_right.shape[2], old_left.dtype
    return pl.pallas_call(
        functools.partial(pick_kernel, factor),
        in_specs=[pl.BlockSpec(memory_space=pltpu.SMEM)] * 2 + [anywhere()] * 3,
        out_specs=[vmem()] * 4,
        out_shape=[
            jax.ShapeDtypeStruct((tall * (slab + wide) // width, width), kind),
            jax.ShapeDtypeStruct((tall, slab), kind),
            jax.ShapeDtypeStruct((tall, wide), kind),
            MARK,
        ],
        scratch_shapes=[
            pltpu.VMEM((chosen, rank, slab), kind),
            pltpu.VMEM((chosen, rank, wide), kind),
            pltpu.SemaphoreType.DMA((2 * chosen,)),
        ],
        compiler_params=pltpu.CompilerParams(vmem_limit_bytes=WIDE),
        cost_estimate=cost(),
    )(selected, shaping, old_left, old_right, after)


def unpack(packed, tall, slab, wide):
    width = packed.shape[1]
    blocks = [slab // width, wide // width]
    got, at = [], 0
    for count in blocks:
        got.append(
            jnp.concatenate([packed[at + tall * i : at + tall * (i + 1)] for i in range(count)], 1)
        )
        at += tall * count
    return got


def mine(shape, rank, each):
    row = lax.broadcasted_iota(jnp.int32, shape, 0)
    token = lax.broadcasted_iota(jnp.int32, shape, 1)
    return lax.div(row, rank) == lax.div(token, each)


def proj_kernel(rank, each, where, left, tok, after, out):
    full = lax.dot_general(
        left[...], tok[...], (((1,), (1,)), ((), ())), preferred_element_type=jnp.float32
    )
    full = jnp.where(mine(full.shape, rank, each), full, 0.0)
    out[...] = full.reshape(-1, *out.shape).sum(0)


def project(tokens, lefts, rank, each, where, after):
    rows, slab = tokens.shape[0], lefts.shape[1]
    return pl.pallas_call(
        functools.partial(proj_kernel, rank, each),
        grid_spec=pltpu.PrefetchScalarGridSpec(
            num_scalar_prefetch=1,
            grid=(1,),
            in_specs=[
                pl.BlockSpec(lefts.shape, lambda k, at: (0, 0)),
                pl.BlockSpec((rows, slab), lambda k, at: (0, at[1])),
                pl.BlockSpec(memory_space=pl.ANY),
            ],
            out_specs=pl.BlockSpec((2 * rank, rows), lambda k, at: (0, 0)),
        ),
        out_shape=jax.ShapeDtypeStruct((2 * rank, rows), jnp.float32),
        compiler_params=params(WIDE),
        cost_estimate=cost(2 * rows * slab * lefts.shape[0], 8 * rows * slab),
    )(where, lefts, tokens, after)


def flipped(index, size):
    got = index * 0
    bit = 1
    while bit < size:
        got = got * 2 + ((index // bit) & 1)
        bit *= 2
    return got


def turn_kernel(where, left, out):
    out[...] = left[...].T


def turn(left, where):
    blocks, sels, slab = left.shape
    return pl.pallas_call(
        turn_kernel,
        grid_spec=pltpu.PrefetchScalarGridSpec(
            num_scalar_prefetch=1,
            grid=(blocks,),
            in_specs=[pl.BlockSpec((None, sels, slab), lambda k, at: (flipped(k ^ at[1], blocks), 0, 0))],
            out_specs=pl.BlockSpec((slab, sels), lambda k, at: (k, 0)),
        ),
        out_shape=jax.ShapeDtypeStruct((blocks * slab, sels), left.dtype),
        compiler_params=params(),
        cost_estimate=cost(),
    )(where, left)


def spread_kernel(rank, each, proj, out):
    narrow = proj[...].astype(jnp.bfloat16).astype(jnp.float32)
    full = jnp.tile(narrow, (out.shape[1] // narrow.shape[0], 1))
    out[...] = jnp.where(mine(full.shape, rank, each), full, 0.0).T.astype(jnp.bfloat16)


def spread_out(proj, members, rank, each):
    return pl.pallas_call(
        functools.partial(spread_kernel, rank, each),
        in_specs=[pl.BlockSpec(memory_space=pltpu.VMEM)],
        out_specs=pl.BlockSpec(memory_space=pltpu.VMEM),
        out_shape=jax.ShapeDtypeStruct((proj.shape[1], members * rank), jnp.bfloat16),
        compiler_params=pltpu.CompilerParams(vmem_limit_bytes=LIMIT),
        cost_estimate=cost(),
    )(proj)


def columns(ref, at, width):
    return ref[:, pl.ds(pl.multiple_of(at * width, width), width)]


def refresh(wt, left, right):
    delta = jnp.dot(left, right, preferred_element_type=jnp.float32)
    return (wt.astype(jnp.float32) + delta).astype(jnp.bfloat16)


def finish(total):
    return (jnp.maximum(total, 0.0) ** 2).astype(jnp.bfloat16)


def begin(scale, spread, rights):
    return scale * jnp.dot(spread, rights, preferred_element_type=jnp.float32)


def full_kernel(scale, keep, begun, where, tok, wt, left, right, spread, rights, *refs):
    out, mark, held = refs[1 if begun else 2], refs[-2], refs[-1]
    step = pl.program_id(0)

    @pl.when(step == 0)
    def _():
        mark[...] = jnp.zeros(MARK.shape, MARK.dtype)
        held[...] = begin(scale, spread[...], rights[...])

    fresh = refresh(wt[...], left[...], right[...])
    if keep:
        refs[-3][...] = fresh
    held[...] += jnp.dot(tok[...], fresh, preferred_element_type=jnp.float32)

    @pl.when(step == pl.num_programs(0) - 1)
    def _():
        out[...] = finish(held[...])


def product(start, where, tok, wt, left, right):
    unit, width = wt.shape
    fresh = refresh(wt[...], left[start : start + unit, :], columns(right, where[0], width))

    def rows(at, size):
        some = tok[at : at + size, start : start + unit]
        return jnp.dot(some, fresh, preferred_element_type=jnp.float32)

    return rows


def sum_kernel(scale, start, where, tok, wt, left, right, *refs):
    out = refs[-1]
    unit, width = wt.shape
    step = pl.program_id(0)

    @pl.when(step == 0)
    def _():
        if start == 0:
            out[...] = begin(scale, refs[0][...], columns(refs[1], where[0], width))
        else:
            out[...] = refs[0][...]

    at = pl.multiple_of(start + step * unit, 128)
    fresh = refresh(wt[...], left[pl.ds(at, unit), :], columns(right, where[0], width))
    out[...] += jnp.dot(tok[:, pl.ds(at, unit)], fresh, preferred_element_type=jnp.float32)


def last_kernel(start, where, tok, wt, left, right, before, acts, out, kept, sems):
    width = wt.shape[1]
    got = product(start, where, tok, wt, left, right)
    part = kept.shape[0] // 4
    place = pl.ds(pl.multiple_of(where[0] * width, width), width)
    copies = []
    for half in range(4):
        rows = pl.ds(half * part, part)
        kept[rows, :] = finish(before[rows, :] + got(half * part, part))
        copies.append(pltpu.make_async_copy(kept.at[rows], out.at[rows, place], sems.at[half]))
        copies[-1].start()
    for copy in copies:
        copy.wait()


def call(
    kernel, where, grid, specs, args, out_specs, out_shape, aliases=None, scratch=(), limit=LIMIT
):
    return pl.pallas_call(
        kernel,
        grid_spec=pltpu.PrefetchScalarGridSpec(
            num_scalar_prefetch=1,
            grid=grid,
            in_specs=specs,
            out_specs=out_specs,
            scratch_shapes=list(scratch),
        ),
        out_shape=out_shape,
        input_output_aliases=aliases or {},
        compiler_params=params(limit),
        cost_estimate=cost(),
    )(where, *args)


def run_block(where, tokens, wt, left, right, start, scale, spread, rights, acts, before, after, keep):
    rows = tokens.shape[0]
    depth, width = wt.shape
    first, last, begun = start == 0, acts is not None, isinstance(acts, tuple)
    tile = pl.BlockSpec((rows, width), lambda k, at: (0, at[0]))
    if first and last:
        unit = depth // 4
        block = pl.BlockSpec((unit, width), lambda k, at: (k, 0))
        specs = [
            pl.BlockSpec((rows, unit), lambda k, at: (0, k)),
            block,
            pl.BlockSpec((unit, left.shape[1]), lambda k, at: (k, 0)),
            pl.BlockSpec((right.shape[0], width), lambda k, at: (0, at[0])),
            pl.BlockSpec(spread.shape, lambda k, at: (0, 0)),
            pl.BlockSpec((rights.shape[0], width), lambda k, at: (0, at[0])),
            anywhere(),
        ]
        args = [tokens, wt, left, right, spread, rights, after]
        aliases = {}
        if not begun:
            specs, args = specs + [anywhere()], args + [acts]
            aliases = {len(args): 0}
        shape = acts if begun else acts.shape
        out_shape, out_specs = [jax.ShapeDtypeStruct(shape, jnp.bfloat16)], [tile]
        if keep:
            out_shape.append(jax.ShapeDtypeStruct((depth, width), jnp.bfloat16))
            out_specs.append(block)
        out_shape.append(MARK)
        out_specs.append(vmem())
        return call(
            functools.partial(full_kernel, scale, keep, begun),
            where, (4,), specs, args, out_specs, out_shape, aliases,
            [pltpu.VMEM((rows, width), jnp.float32)], BROAD,
        )
    if not last:
        extra = [spread, rights] if first else [before]
        unit = depth
        return call(
            functools.partial(sum_kernel, scale, start),
            where, (depth // unit,),
            [vmem(), pl.BlockSpec((unit, width), lambda k, at: (k, 0))]
            + [vmem()] * (2 + len(extra)) + [anywhere()],
            [tokens, wt, left, right, *extra, after], vmem(),
            jax.ShapeDtypeStruct((rows, width), jnp.float32), {} if first else {5: 0},
        )
    return call(
        functools.partial(last_kernel, start),
        where, (1,), [vmem()] * 5 + [anywhere()],
        [tokens, wt, left, right, before, acts], anywhere(),
        jax.ShapeDtypeStruct(acts.shape, jnp.bfloat16), {6: 0},
        [pltpu.VMEM((rows, width), jnp.bfloat16), pltpu.SemaphoreType.DMA((4,))],
    )


def local(tokens, weight, old_left, old_right, selected, shaping, new_left, new_right):
    groups = lax.axis_size("pop")
    me = lax.axis_index("pop")
    spot = lax.axis_index("col")
    depth, width = weight.shape
    members, rank, slab = new_left.shape
    rows = tokens.shape[0]
    each = rows // members
    count = selected.shape[1]
    scale = noise_scale / math.sqrt(depth * rank)
    grain = depth // sum(PIECES)
    chips = groups // 2
    where = jnp.stack([me, spot]).astype(jnp.int32)

    plan = []
    hops = [chips // 2] + [hop for hop in range(1, chips) if hop != chips // 2]
    for hop in hops:
        at = 0
        for piece in PIECES if hop == hops[-1] else (sum(PIECES),):
            plan.append((hop, at * grain, piece * grain))
            at += piece

    def send(index, piece):
        turn = [(p, (p + 2 * plan[index][0]) % groups) for p in range(groups)]
        return lax.ppermute(piece, "pop", turn)

    factor = 1.0 / math.sqrt(depth * rank * count * groups)
    arrived = [send(0, weight[: plan[0][2]])]
    packed, left, right, mark = pick(
        factor, selected, shaping, old_left, old_right, width, selected
    )
    packed = send(0, packed)
    piece, mark = cut(weight, *plan[1][1:], mark)
    arrived.append(send(1, piece))
    tall = count * rank
    arrived[0], mark = gate(arrived[0], mark)
    packed, mark = gate(packed, mark)
    sibling = swap(weight, "pop", 1)
    lefts, rights = unpack(packed, tall, slab, old_right.shape[2])
    left, right = jnp.concatenate([left, lefts], 0), jnp.concatenate([right, rights], 0)
    for bit in bits(chips, 2):
        left = jnp.concatenate([left, swap(left, "pop", bit)], 0)
        right = jnp.concatenate([right, swap(right, "pop", bit)], 0)
    left, mark = gate(left[None], mark)
    rights = new_right.reshape(members * rank, -1)
    proj = project(tokens, new_left.reshape(-1, slab), rank, each, where, mark)
    turns = list(bits(lax.axis_size("col")))[::-1]
    for turn_at, bit in enumerate(turns):
        left = jnp.concatenate([left, swap(left, "col", bit)], 0)
        partial = proj
        proj = proj + swap(proj, "col", bit)
        if turn_at == 0:
            left, right, sibling, mark = gate_all([left, right, sibling], partial)
            right = jnp.concatenate([right, swap(right, "pop", 1)], 0)
            piece, early = cut(weight, *plan[2][1:], mark)
            arrived.append(send(2, piece))
        elif turn_at == 1:
            left, mark = gate(left, partial, early, rights)
            spare, ready = cut(weight, *plan[3][1:], mark)
    left, arrived[1], spare, mark = gate_all([left, arrived[1], spare], partial, ready)
    arrived.append(send(3, spare))
    left = turn(jnp.concatenate([left, swap(left, "pop", 1)], 1), where)
    spread = spread_out(proj, members, rank, each)

    def run(block, wt, start, before, acts, after, keep=False):
        return run_block(
            jnp.reshape(block, (1,)).astype(jnp.int32),
            tokens, wt, left, right, start, scale, spread, rights, acts, before, after, keep,
        )

    narrow = width % 128 != 0
    core = lax.rem(me, 2)

    def pair(own, other):
        return jnp.where(
            core == 0, jnp.concatenate([own, other], 1), jnp.concatenate([other, own], 1)
        )

    whole = (rows, width * groups)
    if narrow:
        acts, both, done = run(me // 2, pair(weight, sibling), 0, None, whole, where, keep=True)
        updated = lax.dynamic_slice_in_dim(both, core * width, width, 1)
    else:
        acts, updated, done = run(me, weight, 0, None, whole, where, keep=True)
    if not narrow:
        acts, done = run(me ^ 1, sibling, 0, None, acts, done)
    many = [index for index, part in enumerate(plan) if part[0] == hops[-1]][:-2]
    for index, (hop, start, size) in enumerate(plan):
        part = arrived[index]
        if index > 1:
            part = hold(part, done)
            arrived[index] = part
            if index + 2 < len(plan):
                part, mark = gate(part, done)
                piece, _ = cut(weight, *plan[index + 2][1:], mark)
                arrived.append(send(index + 2, piece))
        if index in many:
            if index != many[-1]:
                continue
            part = jnp.concatenate([arrived[i] for i in many[:-1]] + [part], 0)
            start, size = 0, part.shape[0]
        other = swap(part, "pop", 1)
        if start == 0:
            sums = [None, None]
        ends = start + size == depth
        source = lax.rem(me - 2 * hop + 2 * groups, groups)
        tasks = ((source, part), (source ^ 1, other))
        if narrow:
            tasks = ((source // 2, pair(part, other)),)
        for side, (block, wt) in enumerate(tasks):
            got = run(block, wt, start, sums[side], acts if ends else None, done)
            if not ends:
                sums[side] = done = got
            elif start == 0:
                acts, done = got
            else:
                acts = got
    return updated, acts


def solution(mesh):
    placed = (
        P("pop", None),
        P(None, ("col", "pop")),
        P("pop", None, "col"),
        P("pop", None, "col"),
        P("pop", None),
        P("pop", None),
        P("pop", None, "col"),
        P("pop", None, "col"),
    )
    return jax.shard_map(
        local,
        mesh=mesh,
        in_specs=placed,
        out_specs=(P(None, ("col", "pop")), P("pop", "col")),
        check_vma=False,
    )
```
